128 devices in a mesh: seq: 8 (over z, core), chan: 16 (over y, x).
Axes of the slice: x: 4, y: 4, z: 4, core: 2. Of those that a mesh axis runs over, the one named last changes fastest.
Arguments:
- x_in: bfloat16 [2048, 8192], P('seq', 'chan'), may hold values from -6 to 6
- z_in: bfloat16 [2048, 8192], P('seq', 'chan'), may hold values from -6 to 6
- grad_out: bfloat16 [2048, 8192], P('seq', 'chan'), may hold values from -6 to 6
- conv_w: float32 [4, 8192], P(None, 'chan'), may hold values from -3 to 3
- conv_b: float32 [8192], P('chan'), may hold values from -3 to 3
- xproj_w: bfloat16 [8192, 288], P('chan'), may hold values from -0.0625 to 0.0625
- dt_w: bfloat16 [256, 8192], P(None, 'chan'), may hold values from -0.375 to 0.375
- dt_bias: float32 [8192], P('chan'), may hold values from -4 to -3
- a_log: float32 [8192, 16], P('chan'), as said below
- d_skip: float32 [8192], P('chan'), may hold values from 0.5 to 1.5
- dt_gain: float32 [256], replicated, may hold values from 0.1 to 1.9
Outputs:
- x_grad: bfloat16 [2048, 8192], P('seq', 'chan')
- z_grad: bfloat16 [2048, 8192], P('seq', 'chan')
- conv_w_grad: float32 [4, 8192], P(None, 'chan')
- conv_b_grad: float32 [8192], P('chan')
- xproj_grad: float32 [8192, 288], P('chan')
- dt_w_grad: float32 [256, 8192], P(None, 'chan')
- dt_bias_grad: float32 [8192], P('chan')
- a_log_grad: float32 [8192, 16], P('chan')
- d_skip_grad: float32 [8192], P('chan')
- dt_gain_grad: float32 [256], replicated
The draws below stay inside these ranges and needn't reach their ends.
Inputs may be any that keep to these rules, and one draw needn't show every extreme that they name: rates -exp(a_log) are spread over channels; their mix depends on the seed.
All inputs are finite; a program needn't handle non-finite values.
Results may differ from the reference program's by a relative error of at most 0.025.
Values may be sent and summed in bfloat16 or wider, within the bound.
A program may use at most 192 MiB of HBM per device.

```python
import math
import jax
import jax.numpy as jnp
from jax import lax

E = 8192
N = 16
K = 4
R = 256
BLOCK = 256
TOKENS = 2048
P_SIZE = 288


def draw_a_log(key, part):
    key = jax.random.fold_in(key, 11)
    pick_key, fast_key, slow_key = jax.random.split(key, 3)
    share = 0.5
    fast = jax.random.uniform(pick_key, (E, 1), jnp.float32) < share
    fast_log = jax.random.uniform(fast_key, (E, N), jnp.float32, -0.69, 0.69)
    slow_rate = jax.random.uniform(slow_key, (E, N), jnp.float32, 0.3, 2.0) / (0.03 * TOKENS)
    return jnp.where(fast, fast_log, jnp.log(slow_rate)).astype(jnp.float32)


def block_scale(stream_key, shape, cuts, smallest, high):
    def one(dim, parts):
        steps = jax.random.uniform(jax.random.fold_in(jax.random.fold_in(stream_key, 6), dim), (parts,), jnp.float32, smallest / len(cuts), high / len(cuts))
        return jnp.repeat(jnp.exp(steps), shape[dim] // parts).reshape((-1,) + (1,) * (len(shape) - dim - 1))

    loudness = one(*cuts[0])
    for cut in cuts[1:]:
        loudness = loudness * one(*cut)
    return loudness


def normal_values(stream_key, extent, width, limit, cuts=(), dtype=jnp.bfloat16):
    drawn = jax.random.normal(stream_key, extent, jnp.float32) * width
    if len(cuts) > 0:
        drawn = block_scale(stream_key, extent, cuts, -0.22, 0.18) * drawn
    return jnp.clip(drawn, min=-limit, max=limit).astype(dtype)


def setup_inputs(seed: int = 0) -> dict:
    key_list = jax.random.split(jax.random.key(seed), 12)
    return {
        "x_in": normal_values(key_list[0], (TOKENS, E), 1.0, 6.0, ((0, 8), (1, 16))),
        "z_in": normal_values(key_list[1], (TOKENS, E), 1.0, 6.0, ((0, 8), (1, 16))),
        "grad_out": normal_values(key_list[2], (TOKENS, E), 1.0, 6.0, ((0, 8), (1, 16))),
        "conv_w": normal_values(key_list[3], (K, E), K ** -0.5, 3.0, ((1, 16),), jnp.float32),
        "conv_b": normal_values(key_list[4], (E,), 0.5, 3.0, ((0, 16),), jnp.float32),
        "xproj_w": normal_values(key_list[5], (E, P_SIZE), E ** -0.5, 0.0625, ((0, 16),)),
        "dt_w": normal_values(key_list[6], (R, E), R ** -0.5, 0.375, ((1, 16),)),
        "dt_bias": jnp.clip(-4.0 + 1.0 * jax.random.uniform(key_list[7], (E,), jnp.float32) ** block_scale(key_list[7], (E,), ((0, 16),), -0.2, 0.2), -4.0, -3.0),
        "a_log": draw_a_log(jax.random.fold_in(key_list[11], 71), 0),
        "d_skip": jnp.clip(0.5 + 1.0 * jax.random.uniform(key_list[9], (E,), jnp.float32) ** block_scale(key_list[9], (E,), ((0, 16),), -0.2, 0.2), 0.5, 1.5),
        "dt_gain": jnp.clip(1.0 + 0.18 * jax.random.normal(key_list[10], (R,), jnp.float32), 0.1, 1.9),
    }


EPS = 1e-06

def silu_grad(value):
    sigma = jax.nn.sigmoid(value)
    return sigma * (1.0 + value * (1.0 - sigma))

def reference(x_in, z_in, grad_out, conv_w, conv_b, xproj_w, dt_w, dt_bias, a_log, d_skip, dt_gain):
    float_t = jnp.float32
    half_t = jnp.bfloat16
    kernel_taps = conv_w.shape[0]
    channels = x_in.shape[1]
    padded = jnp.concatenate([jnp.zeros((kernel_taps - 1, channels), float_t), x_in.astype(float_t)], 0)
    pre_act = conv_b + jnp.zeros((TOKENS, channels), float_t)
    for lag_index in range(kernel_taps):
        pre_act = pre_act + conv_w[lag_index] * padded[lag_index:lag_index + TOKENS]
    gated_in = jax.nn.silu(pre_act).astype(half_t)
    gated_f32 = gated_in.astype(float_t)
    projected = jnp.dot(gated_in, xproj_w, preferred_element_type=float_t)
    dt_low = projected[:, :R]
    b_coef = projected[:, R:R + N]
    c_coef = projected[:, R + N:]
    inv_rms = lax.rsqrt(lax.optimization_barrier(jnp.mean(dt_low * dt_low, -1, keepdims=True)) + EPS)
    dt_normed = (dt_low * inv_rms * dt_gain).astype(half_t)
    pre_soft = jnp.dot(dt_normed, dt_w, preferred_element_type=float_t) + dt_bias
    step_size = jax.nn.softplus(pre_soft)
    decay_rate = -jnp.exp(a_log)
    gate_f32 = z_in.astype(float_t)
    cotangent = grad_out.astype(float_t)
    out_grad = cotangent * jax.nn.silu(gate_f32)
    drive = step_size * gated_f32
    block_count = TOKENS // BLOCK

    def blocked(array):
        return array.reshape((block_count, BLOCK) + array.shape[1:])

    def advance(state_now, pieces):
        steps, drives, b_rows = pieces
        return (jnp.exp(steps[:, None] * decay_rate) * state_now + drives[:, None] * b_rows[None, :], None)

    def run_block(state_now, pieces):
        ending, _ = lax.scan(advance, state_now, pieces)
        return (ending, state_now)
    zero_state = jnp.zeros((channels, N), float_t)
    _, starts = lax.scan(run_block, zero_state, (blocked(step_size), blocked(drive), blocked(b_coef)))

    def record(state_now, pieces):
        steps, drives, b_rows = pieces
        following = jnp.exp(steps[:, None] * decay_rate) * state_now + drives[:, None] * b_rows[None, :]
        return (following, state_now)

    def retreat(carry, pieces):
        ahead, grad_decay = carry
        previous, steps, drives, gated, b_rows, c_rows, grads = pieces
        decay = jnp.exp(steps[:, None] * decay_rate)
        current = decay * previous + drives[:, None] * b_rows[None, :]
        adjoint = c_rows[None, :] * grads[:, None] + ahead
        adjoint_b = lax.optimization_barrier(jnp.sum(adjoint * b_rows[None, :], 1))
        hold = adjoint * previous * decay
        y_row = lax.optimization_barrier(jnp.sum(current * c_rows[None, :], 1)) + d_skip * gated
        c_grad = lax.optimization_barrier(jnp.sum(current * grads[:, None], 0))
        b_grad = lax.optimization_barrier(jnp.sum(adjoint * drives[:, None], 0))
        step_grad = lax.optimization_barrier(jnp.sum(hold * decay_rate, 1)) + adjoint_b * gated
        gated_grad = d_skip * grads + steps * adjoint_b
        grad_decay = grad_decay + hold * steps[:, None]
        return ((decay * adjoint, grad_decay), (y_row, b_grad, c_grad, step_grad, gated_grad))

    def back_block(carry, pieces):
        start, steps, drives, gated, b_rows, c_rows, grads = pieces
        _, previous = lax.scan(record, start, (steps, drives, b_rows))
        return lax.scan(retreat, carry, (previous, steps, drives, gated, b_rows, c_rows, grads), reverse=True)
    (_, grad_decay), stacked = lax.scan(back_block, (zero_state, zero_state), (starts, blocked(step_size), blocked(drive), blocked(gated_f32), blocked(b_coef), blocked(c_coef), blocked(out_grad)), reverse=True)
    y_rows, b_grad, c_grad, step_grad, gated_grad = [piece.reshape((TOKENS,) + piece.shape[2:]) for piece in stacked]
    z_grad = (cotangent * y_rows * silu_grad(gate_f32)).astype(half_t)
    pre_grad = step_grad * jax.nn.sigmoid(pre_soft)
    pre_half = pre_grad.astype(half_t)
    normed_grad = jnp.dot(pre_half, dt_w.T, preferred_element_type=float_t)
    scaled = normed_grad * dt_gain
    low_grad = inv_rms * scaled - dt_low * inv_rms * inv_rms * inv_rms * lax.optimization_barrier(jnp.mean(scaled * dt_low, -1, keepdims=True))
    gain_grad = lax.optimization_barrier(jnp.sum(normed_grad * dt_low * inv_rms, 0))
    proj_grad = jnp.concatenate([low_grad, b_grad, c_grad], 1).astype(half_t)
    gated_total = gated_grad + jnp.dot(proj_grad, xproj_w.T, preferred_element_type=float_t)
    xproj_grad = jnp.dot(gated_in.T, proj_grad, preferred_element_type=float_t)
    dtw_grad = jnp.dot(dt_normed.T, pre_half, preferred_element_type=float_t)
    act_grad = gated_total * silu_grad(pre_act)
    extended = jnp.concatenate([act_grad, jnp.zeros((kernel_taps - 1, channels), float_t)], 0)
    x_grad = jnp.zeros((TOKENS, channels), float_t)
    for lag_index in range(kernel_taps):
        begin = kernel_taps - 1 - lag_index
        x_grad = x_grad + conv_w[lag_index] * extended[begin:begin + TOKENS]
    conv_grad = jnp.stack([lax.optimization_barrier(jnp.sum(act_grad * padded[lag_index:lag_index + TOKENS], 0)) for lag_index in range(kernel_taps)], 0)
    scale = 1.0 / math.sqrt(TOKENS)
    return (x_grad.astype(half_t), z_grad, scale * conv_grad, scale * lax.optimization_barrier(jnp.sum(act_grad, 0)), scale * xproj_grad, scale * dtw_grad, scale * lax.optimization_barrier(jnp.sum(pre_grad, 0)), scale * grad_decay * decay_rate, scale * lax.optimization_barrier(jnp.sum(out_grad * gated_f32, 0)), scale * gain_grad)
```

```python
import functools
import math

import jax
import jax.numpy as jnp
from jax import lax
from jax.experimental import pallas as pl
from jax.experimental.pallas import tpu as pltpu
from jax.sharding import PartitionSpec as P

EPS = 1e-06
LOG2E = 1.4426950408889634
LANES = 128
GROUP = 16
F32 = jnp.float32
BF16 = jnp.bfloat16
MESH = pl.DeviceIdType.MESH


def dot(a, b):
    return jnp.dot(a, b, preferred_element_type=F32)


def dot_nt(a, b):
    return lax.dot_general(a, b, (((1,), (1,)), ((), ())), preferred_element_type=F32)


def iota(shape, dim):
    return lax.broadcasted_iota(jnp.int32, shape, dim)


def silu_grad(value):
    sigma = jax.nn.sigmoid(value)
    return sigma * (1.0 + value * (1.0 - sigma))


def softplus(value):
    return jnp.maximum(value, 0.0) + jnp.log1p(jnp.exp(-jnp.abs(value)))


class Exchange:
    def __init__(self, axis, count, me, send_sem, recv_sem):
        self.axis, self.count, self.me = axis, count, me
        self.send_sem, self.recv_sem = send_sem, recv_sem

    def _copy(self, src, dst, send, recv, peer):
        return pltpu.make_async_remote_copy(
            src_ref=src,
            dst_ref=dst,
            send_sem=self.send_sem.at[send],
            recv_sem=self.recv_sem.at[recv],
            device_id={self.axis: peer},
            device_id_type=MESH,
        )

    def peers(self):
        return [lax.rem(self.me + d, self.count) for d in range(1, self.count)]

    def send(self, src, dst, peer):
        self._copy(src, dst, peer, self.me, peer).start()

    def wait_recv(self, slot, peer):
        self._copy(slot, slot, peer, peer, peer).wait_recv()

    def wait_send(self, slot, peer):
        self._copy(slot, slot, peer, peer, peer).wait_send()


def layer_kernel(dims, *refs):
    T, C, NS, NC, R, N = dims
    (x_ref, z_ref, g_ref, cw_ref, cb_ref, xw_ref, dw_ref, db_ref, al_ref, ds_ref, dg_ref,
     xg_o, zg_o, cwg_o, cbg_o, xpg_o, dwg_o, dbg_o, alg_o, dsg_o, dgg_o,
     xpad, pre_act, u_bf, ut_bf, gy, gz, xwp, part, send1, rs1, ag1, low_own, inv_own,
     pre_soft, delta, drive, bB, cB, a_buf, h_buf, lam_buf, ha_buf,
     st_f, st_b, tot, in_f, in_b, in_tot, carry_f, carry_b,
     e_exp, m_b, m_c, sel_b, sel_c, dmask, back_b, back_c,
     yv, bcg, uscan, pregrad, prehalf, send2, rs2, ag2,
     dw_f, dw_send, dw_rs, dw_ag, xl_f, xl_send, xl_rs, xl_ag, sm_f, sm_rs, sm_ag,
     halo_x, halo_a, apad,
     s_c, r_c, s_st, r_st, s_sq, r_sq, s_h, r_h) = refs
    ROWS = T // NC
    W = R + LANES
    NB = T // GROUP
    GN = GROUP * N
    RB, CB = R // NS, C // NS
    SM = sm_f.shape[0]
    SB = SM // NS
    ms, mc = lax.axis_index("seq"), lax.axis_index("chan")

    def chan(k):
        return Exchange("chan", NC, mc, s_c.at[k], r_c.at[k])

    def seq(k):
        return Exchange("seq", NS, ms, s_sq.at[k], r_sq.at[k])

    def states(k):
        return Exchange("seq", NS, ms, s_st.at[k], r_st.at[k])

    barrier = pltpu.get_barrier_semaphore()
    for d in range(1, NC):
        pl.semaphore_signal(barrier, inc=1, device_id={"chan": lax.rem(mc + d, NC)}, device_id_type=MESH)
    for d in range(1, NS):
        pl.semaphore_signal(barrier, inc=1, device_id={"seq": lax.rem(ms + d, NS)}, device_id_type=MESH)

    e_exp[...] = (iota((GN, GROUP), 0) // N == iota((GN, GROUP), 1)).astype(F32).astype(BF16)
    row_n, lane = iota((GN, LANES), 0) % N, iota((GN, LANES), 1)
    m_b[...] = ((lane == row_n) | (lane == row_n + 2 * N)).astype(F32)
    m_c[...] = ((lane == row_n + N) | (lane == row_n + 3 * N)).astype(F32)
    back_b[...] = (lane == row_n).astype(F32).astype(BF16)
    back_c[...] = (lane == row_n + N).astype(F32).astype(BF16)
    k_row, col_n = iota((LANES, GN), 0), iota((LANES, GN), 1) % N
    sel_b[...] = ((k_row == col_n) | (k_row == col_n + 2 * N)).astype(F32).astype(BF16)
    sel_c[...] = ((k_row == col_n + N) | (k_row == col_n + 3 * N)).astype(F32).astype(BF16)
    dmask[...] = (iota((GROUP, GN), 1) // N == iota((GROUP, GN), 0)).astype(F32)
    xwp[...] = jnp.zeros_like(xwp)
    xwp[:, : R + 2 * N] = xw_ref[...]

    xpad[:8, :] = jnp.zeros((8, C), F32)
    xpad[8:, :] = x_ref[...].astype(F32)
    cw = cw_ref[...]

    def conv(first, count):
        total = jnp.broadcast_to(cb_ref[...], (count, C))
        for k in range(4):
            total = total + cw[k : k + 1] * xpad[first + 5 + k : first + 5 + k + count, :]
        return total

    pre_act[...] = conv(0, T)
    pl.semaphore_wait(barrier, NC + NS - 2)
    halo = Exchange("seq", NS, ms, s_h, r_h)

    def halo_copy(src, dst, k, peer):
        return pltpu.make_async_remote_copy(
            src_ref=src, dst_ref=dst, send_sem=s_h.at[k], recv_sem=r_h.at[k],
            device_id={"seq": peer}, device_id_type=MESH,
        )

    after, before = lax.rem(ms + 1, NS), lax.rem(ms + NS - 1, NS)

    @pl.when(ms < NS - 1)
    def _():
        halo_copy(x_ref.at[T - 16 :, :], halo_x, 0, after).start()

    gate = z_ref[...].astype(F32)
    cot = g_ref[...].astype(F32)
    sig = jax.nn.sigmoid(gate)
    gy[...] = cot * gate * sig
    gz[...] = cot * sig * (1.0 + gate * (1.0 - sig))

    @pl.when(ms > 0)
    def _():
        halo_copy(halo_x, halo_x, 0, before).wait_recv()
        xpad[:8, :] = halo_x[...].astype(F32)[8:16]
        pre_act[:8, :] = conv(0, 8)

    act = pre_act[...]
    u_bf[...] = (act * jax.nn.sigmoid(act)).astype(BF16)

    part[...] = dot(u_bf[...], xwp[...])
    send1[...] = part[...].astype(BF16)

    def my_rows(ref):
        return ref[pl.ds(pl.multiple_of(mc * ROWS, ROWS), ROWS), :]

    def block(ref, i, size):
        return ref.at[pl.ds(pl.multiple_of(i * size, size), size), :]

    def scatter(ex, src, slots, size):
        for peer in ex.peers():
            ex.send(block(src, peer, size), slots.at[ex.me], peer)

    def collect(ex, slots, own):
        for peer in ex.peers():
            ex.wait_recv(slots.at[peer], peer)
        for peer in ex.peers():
            own = own + slots[peer].astype(F32)
        return own

    def spread(ex, buf, size):
        for peer in ex.peers():
            ex.send(block(buf, ex.me, size), block(buf, ex.me, size), peer)

    def arrive(ex, buf, size):
        for peer in ex.peers():
            ex.wait_recv(block(buf, peer, size), peer)

    scatter(chan(0), send1, rs1, ROWS)
    ut_bf[...] = u_bf[...].astype(F32).T.astype(BF16)
    rate = -jnp.exp(al_ref[...].T)
    rate2 = rate * LOG2E
    proj = collect(chan(0), rs1, my_rows(part))
    low = proj[:, :R]
    inv = lax.rsqrt(jnp.mean(low * low, -1, keepdims=True) + EPS)
    low_own[...] = low
    inv_own[...] = jnp.broadcast_to(inv, inv_own.shape)
    tail = proj[:, R:]
    tail_hi = tail.astype(BF16).astype(F32)
    tail = tail_hi + pltpu.roll(tail - tail_hi, 2 * N, 1)
    mine = pl.ds(pl.multiple_of(mc * ROWS, ROWS), ROWS)
    ag1[mine, :R] = (low * inv * dg_ref[...]).astype(BF16)
    ag1[mine, R:] = tail.astype(BF16)
    spread(chan(1), ag1, ROWS)
    arrive(chan(1), ag1, ROWS)

    soft = dot(ag1[:, :R], dw_ref[...]) + db_ref[...]
    pre_soft[...] = soft
    step = softplus(soft)
    delta[...] = step
    drive[...] = step * u_bf[...].astype(F32)
    tot[...] = jnp.sum(step, 0, keepdims=True)
    for peer in states(2).peers():
        states(2).send(tot, in_tot.at[ms], peer)

    ones = jnp.ones((LANES, LANES), BF16)

    def widen(i, carry):
        rows = ag1[pl.ds(pl.multiple_of(i * GROUP, GROUP), GROUP), R:]
        spread_rows = dot(e_exp[...], rows)
        at = pl.ds(pl.multiple_of(i * GN, GN), GN)
        bB[at, :] = dot((spread_rows * m_b[...]).astype(BF16), ones)
        cB[at, :] = dot((spread_rows * m_c[...]).astype(BF16), ones)
        return carry

    lax.fori_loop(0, NB, widen, 0)

    def row(ref, t):
        return ref[pl.ds(t, 1), :]

    def state_at(t):
        return pl.ds(pl.multiple_of(t * N, N), N)

    def wide(ref, t):
        return jnp.concatenate([ref[state_at(t), :]] * (C // LANES), axis=1)

    zero_state = jnp.zeros((N, C), F32)

    def forward_part(i, h):
        for j in range(GROUP):
            t = i * GROUP + j
            a = jnp.exp2(row(delta, t) * rate2)
            a_buf[state_at(t), :] = a
            h = a * h + row(drive, t) * wide(bB, t)
        return h

    st_f[...] = lax.fori_loop(0, NB, forward_part, zero_state).astype(BF16)
    for d in range(1, NS):

        @pl.when(ms + d < NS)
        def _(d=d):
            states(0).send(st_f, in_f.at[ms], ms + d)

    def backward_part(i, g):
        for j in range(GROUP):
            t = T - 1 - (i * GROUP + j)
            g = a_buf[state_at(t), :] * (row(gy, t) * wide(cB, t) + g)
        return g

    st_b[...] = lax.fori_loop(0, NB, backward_part, zero_state).astype(BF16)
    for d in range(1, NS):

        @pl.when(ms - d >= 0)
        def _(d=d):
            states(1).send(st_b, in_b.at[ms], ms - d)

    for peer in states(2).peers():
        states(2).wait_recv(in_tot.at[peer], peer)
    carry_f[...] = zero_state
    for s in range(NS - 1):

        @pl.when(s < ms)
        def _(s=s):
            states(0).wait_recv(in_f.at[s], s)
            carry_f[...] = jnp.exp2(in_tot[s] * rate2) * carry_f[...] + in_f[s].astype(F32)

    start = carry_f[...]
    h_buf[:N, :] = start.astype(BF16)

    def forward(i, h):
        for j in range(GROUP):
            t = i * GROUP + j
            h = a_buf[state_at(t), :] * h + row(drive, t) * wide(bB, t)
            h_buf[state_at(t + 1), :] = h.astype(BF16)
        return h

    lax.fori_loop(0, NB, forward, start)

    def tokens(i):
        return pl.ds(pl.multiple_of(i * GROUP, GROUP), GROUP)

    def after_forward(i, carry):
        coef = ag1[tokens(i), R:]
        h_rows = h_buf[pl.ds(pl.multiple_of(i * GN + N, N), GN), :]
        c_diag = (dot(coef, sel_c[...]) * dmask[...]).astype(BF16)
        yv[tokens(i), :] = dot(c_diag, h_rows)
        c_all = dot_nt(gy[tokens(i), :].astype(BF16), h_rows) * dmask[...]
        bcg[tokens(i), :] = dot(c_all.astype(BF16), back_c[...])
        return carry

    lax.fori_loop(0, NB, after_forward, 0)

    carry_b[...] = zero_state
    for s in range(NS - 1, 0, -1):

        @pl.when(s > ms)
        def _(s=s):
            states(1).wait_recv(in_b.at[s], s)
            carry_b[...] = jnp.exp2(in_tot[s] * rate2) * carry_b[...] + in_b[s].astype(F32)

    def backward(i, carry):
        g, acc = carry
        for j in range(GROUP):
            t = T - 1 - (i * GROUP + j)
            lam = row(gy, t) * wide(cB, t) + g
            g = a_buf[state_at(t), :] * lam
            hold = g * h_buf[state_at(t), :].astype(F32)
            acc = acc + hold * row(delta, t)
            lam_buf[state_at(t), :] = lam.astype(BF16)
            ha_buf[state_at(t), :] = (hold * rate).astype(BF16)
        return g, acc

    _, rate_sum = lax.fori_loop(0, NB, backward, (carry_b[...], zero_state))

    def after_backward(i, carry):
        coef = ag1[tokens(i), R:]
        at = pl.ds(pl.multiple_of(i * GN, GN), GN)
        lam_rows = lam_buf[at, :]
        b_diag = (dot(coef, sel_b[...]) * dmask[...]).astype(BF16)
        adj_b = dot(b_diag, lam_rows)
        by_rate = dot(dmask[...].astype(BF16), ha_buf[at, :])
        b_all = dot_nt(drive[tokens(i), :].astype(BF16), lam_rows) * dmask[...]
        bcg[tokens(i), :] = bcg[tokens(i), :] + dot(b_all.astype(BF16), back_b[...])
        pre = (by_rate + adj_b * u_bf[tokens(i), :].astype(F32)) * jax.nn.sigmoid(pre_soft[tokens(i), :])
        pregrad[tokens(i), :] = pre
        prehalf[tokens(i), :] = pre.astype(BF16)
        uscan[tokens(i), :] = ds_ref[...] * gy[tokens(i), :] + delta[tokens(i), :] * adj_b
        return carry

    lax.fori_loop(0, NB, after_backward, 0)

    part[:, :R] = dot_nt(prehalf[...], dw_ref[...])
    part[:, R:] = bcg[...]
    send2[...] = part[...].astype(BF16)
    scatter(chan(2), send2, rs2, ROWS)

    dw_f[...] = dot(ag1[:, :R].astype(F32).T.astype(BF16), prehalf[...])
    dw_send[...] = dw_f[...].astype(BF16)
    scatter(seq(0), dw_send, dw_rs, RB)
    u32 = u_bf[...].astype(F32)
    zg_o[...] = (gz[...] * (yv[...] + ds_ref[...] * u32)).astype(BF16)
    sm_f[...] = jnp.zeros_like(sm_f)
    sm_f[2 * N : 3 * N, :] = rate_sum * rate
    sm_f[3 * N + 5 : 3 * N + 6, :] = jnp.sum(pregrad[...], 0, keepdims=True)
    sm_f[3 * N + 6 : 3 * N + 7, :] = jnp.sum(gy[...] * u32, 0, keepdims=True)

    grad_rows = collect(chan(2), rs2, my_rows(part))
    low = low_own[...]
    inv = inv_own[:, :1]
    scaled = grad_rows[:, :R] * dg_ref[...]
    low_grad = inv * scaled - low * (inv * inv * inv) * jnp.mean(scaled * low, -1, keepdims=True)
    gain = jnp.sum(grad_rows[:, :R] * low * inv, 0, keepdims=True)
    half = LANES // 2
    lanes = iota((ROWS, LANES), 1)
    rows = iota((ROWS, LANES), 0)
    g0 = jnp.broadcast_to(gain[:, :LANES], (ROWS, LANES))
    g1 = jnp.broadcast_to(gain[:, LANES:], (ROWS, LANES))
    q = rows % 4
    gq = jnp.where(q == 0, pltpu.roll(g0, half, 1), jnp.where(q == 1, g0, jnp.where(q == 2, pltpu.roll(g1, half, 1), g1)))
    g_hi = gq.astype(BF16).astype(F32)
    g_rows = jnp.where(rows < 4, g_hi, jnp.where(rows < 8, gq - g_hi, 0.0))
    ag2[mine, :R] = low_grad.astype(BF16)
    ag2[mine, R:] = jnp.where(lanes < half, grad_rows[:, R:], g_rows).astype(BF16)
    spread(chan(3), ag2, ROWS)

    own = collect(seq(0), dw_rs, dw_f[pl.ds(pl.multiple_of(ms * RB, RB), RB), :])
    dw_ag[pl.ds(pl.multiple_of(ms * RB, RB), RB), :] = own.astype(BF16)
    spread(seq(1), dw_ag, RB)

    arrive(chan(3), ag2, ROWS)
    keep = iota((T, W), 1) < R + 2 * N
    pg = jnp.where(keep, ag2[...].astype(F32), 0.0).astype(BF16)
    act = pre_act[...]
    total = uscan[...] + dot_nt(pg, xwp[...])
    act_grad = total * silu_grad(act)
    apad[:T, :] = act_grad
    apad[T:, :] = jnp.zeros((8, C), F32)

    @pl.when(ms > 0)
    def _():
        halo_copy(apad.at[:8, :], halo_a, 1, before).start()

    xl_f[...] = dot(ut_bf[...], pg[:, :R])
    xl_send[...] = xl_f[...].astype(BF16)
    scatter(seq(2), xl_send, xl_rs, CB)
    sm_f[: 2 * N, :] = dot(pg[:, R:].astype(F32).T.astype(BF16), u_bf[...])[: 2 * N]
    for k in range(4):
        sm_f[3 * N + k : 3 * N + k + 1, :] = jnp.sum(act_grad * xpad[5 + k : 5 + k + T, :], 0, keepdims=True)
    sm_f[3 * N + 4 : 3 * N + 5, :] = jnp.sum(act_grad, 0, keepdims=True)
    g_sum = jnp.zeros((ROWS, LANES), F32)
    for c in range(NC):
        g_sum = g_sum + ag2[c * ROWS : (c + 1) * ROWS, R:].astype(F32)
    gq = g_sum[:4] + g_sum[4:8]
    low_half = iota((1, LANES), 1) < half
    for k in range(2):
        sm_f[3 * N + 7 : 3 * N + 8, k * LANES : (k + 1) * LANES] = jnp.where(
            low_half, pltpu.roll(gq[2 * k : 2 * k + 1], half, 1), gq[2 * k + 1 : 2 * k + 2]
        )
    scatter(seq(3), sm_f, sm_rs, SB)

    @pl.when(ms < NS - 1)
    def _():
        halo_copy(halo_a, halo_a, 1, after).wait_recv()
        apad[T:, :] = halo_a[...]

    total = jnp.zeros((T, C), F32)
    for k in range(4):
        total = total + cw[k : k + 1] * apad[3 - k : 3 - k + T, :]
    xg_o[...] = total.astype(BF16)

    scale = 1.0 / math.sqrt(T * NS)
    at = pl.ds(pl.multiple_of(ms * CB, CB), CB)
    xl_ag[at, :] = collect(seq(2), xl_rs, xl_f[at, :]).astype(BF16)
    spread(seq(4), xl_ag, CB)
    at = pl.ds(pl.multiple_of(ms * SB, SB), SB)
    sm_ag[at, :] = collect(seq(3), sm_rs, sm_f[at, :])
    spread(seq(5), sm_ag, SB)
    arrive(seq(1), dw_ag, RB)
    dwg_o[...] = scale * dw_ag[...].astype(F32)
    arrive(seq(4), xl_ag, CB)
    xpg_o[:, :R] = scale * xl_ag[...].astype(F32)
    arrive(seq(5), sm_ag, SB)
    small = scale * sm_ag[...]
    flipped = small.T
    xpg_o[:, R:] = flipped[:, : 2 * N]
    alg_o[...] = flipped[:, 2 * N : 3 * N]
    cwg_o[...] = small[3 * N : 3 * N + 4]
    cbg_o[...] = small[3 * N + 4 : 3 * N + 5]
    dbg_o[...] = small[3 * N + 5 : 3 * N + 6]
    dsg_o[...] = small[3 * N + 6 : 3 * N + 7]
    dgg_o[...] = small[3 * N + 7 : 3 * N + 8, :R]

    for k, size, src in ((0, ROWS, send1), (1, ROWS, ag1), (2, ROWS, send2), (3, ROWS, ag2)):
        for peer in chan(k).peers():
            chan(k).wait_send(src.at[:size, :], peer)
    for k, size, src in ((0, RB, dw_send), (1, RB, dw_ag), (2, CB, xl_send), (3, SB, sm_f), (4, CB, xl_ag), (5, SB, sm_ag)):
        for peer in seq(k).peers():
            seq(k).wait_send(src.at[:size, :], peer)
    for peer in states(2).peers():
        states(2).wait_send(tot, peer)
    for d in range(1, NS):

        @pl.when(ms + d < NS)
        def _(d=d):
            states(0).wait_send(st_f, ms + d)

        @pl.when(ms - d >= 0)
        def _(d=d):
            states(1).wait_send(st_b, ms - d)

    @pl.when(ms < NS - 1)
    def _():
        halo_copy(halo_x, halo_x, 0, after).wait_send()

    @pl.when(ms > 0)
    def _():
        halo_copy(halo_a, halo_a, 1, before).wait_send()


def per_device(counts, x_in, z_in, grad_out, conv_w, conv_b, xproj_w, dt_w, dt_bias, a_log, d_skip, dt_gain):
    T, C = x_in.shape
    R = dt_w.shape[0]
    N = a_log.shape[1]
    NS, NC = counts
    ROWS = T // NC
    W = R + LANES
    GN = GROUP * N
    SM = 4 * N
    dims = (T, C, NS, NC, R, N)

    def f32(*shape):
        return pltpu.VMEM(shape, F32)

    def b16(*shape):
        return pltpu.VMEM(shape, BF16)

    dma = pltpu.SemaphoreType.DMA
    scratch = dict(
        xpad=f32(T + 8, C), pre_act=f32(T, C), u_bf=b16(T, C), ut_bf=b16(C, T), gy=f32(T, C), gz=f32(T, C),
        xwp=b16(C, W), part=f32(T, W), send1=b16(T, W), rs1=b16(NC, ROWS, W), ag1=b16(T, W),
        low_own=f32(ROWS, R), inv_own=f32(ROWS, LANES),
        pre_soft=f32(T, C), delta=f32(T, C), drive=f32(T, C), bB=f32(T * N, LANES), cB=f32(T * N, LANES),
        a_buf=f32(T * N, C), h_buf=b16((T + 1) * N, C), lam_buf=b16(T * N, C), ha_buf=b16(T * N, C),
        st_f=b16(N, C), st_b=b16(N, C), tot=f32(1, C), in_f=b16(NS, N, C), in_b=b16(NS, N, C),
        in_tot=f32(NS, 1, C), carry_f=f32(N, C), carry_b=f32(N, C),
        e_exp=b16(GN, GROUP), m_b=f32(GN, LANES), m_c=f32(GN, LANES), sel_b=b16(LANES, GN), sel_c=b16(LANES, GN),
        dmask=f32(GROUP, GN), back_b=b16(GN, LANES), back_c=b16(GN, LANES),
        yv=f32(T, C), bcg=f32(T, LANES), uscan=f32(T, C), pregrad=f32(T, C), prehalf=b16(T, C),
        send2=b16(T, W), rs2=b16(NC, ROWS, W), ag2=b16(T, W),
        dw_f=f32(R, C), dw_send=b16(R, C), dw_rs=b16(NS, R // NS, C), dw_ag=b16(R, C),
        xl_f=f32(C, R), xl_send=b16(C, R), xl_rs=b16(NS, C // NS, R), xl_ag=b16(C, R),
        sm_f=f32(SM, C), sm_rs=f32(NS, SM // NS, C), sm_ag=f32(SM, C),
        halo_x=b16(16, C), halo_a=f32(8, C), apad=f32(T + 8, C),
        s_c=dma((4, NC)), r_c=dma((4, NC)), s_st=dma((3, NS)), r_st=dma((3, NS)),
        s_sq=dma((6, NS)), r_sq=dma((6, NS)), s_h=dma((2,)), r_h=dma((2,)),
    )
    S = jax.ShapeDtypeStruct
    out_shape = (
        S((T, C), BF16), S((T, C), BF16), S((4, C), F32), S((1, C), F32), S((C, R + 2 * N), F32),
        S((R, C), F32), S((1, C), F32), S((C, N), F32), S((1, C), F32), S((1, R), F32),
    )
    vmem = pl.BlockSpec(memory_space=pltpu.VMEM)
    out = pl.pallas_call(
        functools.partial(layer_kernel, dims),
        out_shape=out_shape,
        in_specs=[vmem] * 11,
        out_specs=(vmem,) * 10,
        scratch_shapes=list(scratch.values()),
        compiler_params=pltpu.CompilerParams(
            collective_id=0, has_side_effects=True, vmem_limit_bytes=60 * 1024 * 1024
        ),
    )(
        x_in, z_in, grad_out, conv_w, conv_b[None], xproj_w, dt_w, dt_bias[None], a_log, d_skip[None], dt_gain[None],
    )
    xg, zg, cwg, cbg, xpg, dwg, dbg, alg, dsg, dgg = out
    return xg, zg, cwg, cbg[0], xpg, dwg, dbg[0], alg, dsg[0], dgg[0]


def solution(mesh):
    placed = (
        P("seq", "chan"),
        P("seq", "chan"),
        P("seq", "chan"),
        P(None, "chan"),
        P("chan"),
        P("chan", None),
        P(None, "chan"),
        P("chan"),
        P("chan", None),
        P("chan"),
        P(),
    )
    counts = (mesh.shape["seq"], mesh.shape["chan"])
    return jax.shard_map(
        functools.partial(per_device, counts),
        mesh=mesh,
        in_specs=placed,
        out_specs=(
            P("seq", "chan"),
            P("seq", "chan"),
            P(None, "chan"),
            P("chan"),
            P("chan", None),
            P(None, "chan"),
            P("chan"),
            P("chan", None),
            P("chan"),
            P(),
        ),
        check_vma=False,
    )
```

```python
import functools
import math

import jax
import jax.numpy as jnp
from jax import lax
from jax.experimental import pallas as pl
from jax.experimental.pallas import tpu as pltpu
from jax.sharding import PartitionSpec as P

EPS = 1e-06
LOG2E = 1.4426950408889634
LANES = 128
GROUP = 16
F32 = jnp.float32
BF16 = jnp.bfloat16
MESH = pl.DeviceIdType.MESH
VMEM_BYTES = 60 * 1024 * 1024


def dot(a, b):
    return jnp.dot(a, b, preferred_element_type=F32)


def dot_nt(a, b):
    return lax.dot_general(a, b, (((1,), (1,)), ((), ())), preferred_element_type=F32)


def dot_tn(a, b):
    return lax.dot_general(a, b, (((0,), (0,)), ((), ())), preferred_element_type=F32)


def iota(shape, dim):
    return lax.broadcasted_iota(jnp.int32, shape, dim)


def silu_grad(value):
    sigma = jax.nn.sigmoid(value)
    return sigma * (1.0 + value * (1.0 - sigma))


def softplus(value):
    return jnp.maximum(value, 0.0) + jnp.log1p(jnp.exp(-jnp.abs(value)))


class Exchange:
    def __init__(self, axis, count, me, send_sem, recv_sem):
        self.axis, self.count, self.me = axis, count, me
        self.send_sem, self.recv_sem = send_sem, recv_sem

    def _copy(self, src, dst, send, recv, peer):
        return pltpu.make_async_remote_copy(
            src_ref=src,
            dst_ref=dst,
            send_sem=self.send_sem.at[send],
            recv_sem=self.recv_sem.at[recv],
            device_id={self.axis: peer},
            device_id_type=MESH,
        )

    def peers(self):
        return [lax.rem(self.me + d, self.count) for d in range(1, self.count)]

    def send(self, src, dst, peer):
        self._copy(src, dst, peer, self.me, peer).start()

    def wait_recv(self, slot, peer):
        self._copy(slot, slot, peer, peer, peer).wait_recv()

    def wait_send(self, slot, peer):
        self._copy(slot, slot, peer, peer, peer).wait_send()


def layer_kernel(dims, *refs):
    T, C, NS, NC, R, N = dims
    (x_ref, z_ref, g_ref, cw_ref, cb_ref, xw_ref, dw_ref, db_ref, al_ref, ds_ref, dg_ref,
     xg_o, zg_o, dw_ag, xl_ag, sm_ag,
     xpad, pre_act, u_bf, gy, gz, xwp, part, send1, rs1, ag1, low_own, inv_own,
     pre_soft, delta, drive, bB, cB, a_buf, h_buf, lam_buf, ha_buf,
     st_f, st_b, tot, in_f, in_b, in_tot, carry_f, carry_b,
     e_exp, m_b, m_c, sel_b, sel_c, dmask, back_b, back_c,
     yv, bcg, uscan, pregrad, prehalf, send2, rs2, ag2,
     dw_f, dw_send, dw_rs, xl_f, xl_send, xl_rs, sm_f, sm_rs,
     halo_x, halo_a, apad,
     s_c, r_c, s_st, r_st, s_sq, r_sq, s_h, r_h) = refs
    ROWS = T // NC
    W = R + LANES
    NB = T // GROUP
    GN = GROUP * N
    RB = R // NS
    SM = sm_f.shape[0]
    SB = SM // NS
    ms, mc = lax.axis_index("seq"), lax.axis_index("chan")

    def chan(k):
        return Exchange("chan", NC, mc, s_c.at[k], r_c.at[k])

    def seq(k):
        return Exchange("seq", NS, ms, s_sq.at[k], r_sq.at[k])

    def states(k):
        return Exchange("seq", NS, ms, s_st.at[k], r_st.at[k])

    barrier = pltpu.get_barrier_semaphore()
    for d in range(1, NC):
        pl.semaphore_signal(barrier, inc=1, device_id={"chan": lax.rem(mc + d, NC)}, device_id_type=MESH)
    for d in range(1, NS):
        pl.semaphore_signal(barrier, inc=1, device_id={"seq": lax.rem(ms + d, NS)}, device_id_type=MESH)

    e_exp[...] = (iota((GN, GROUP), 0) // N == iota((GN, GROUP), 1)).astype(F32).astype(BF16)
    row_n, lane = iota((GN, LANES), 0) % N, iota((GN, LANES), 1)
    m_b[...] = ((lane == row_n) | (lane == row_n + 2 * N)).astype(F32)
    m_c[...] = ((lane == row_n + N) | (lane == row_n + 3 * N)).astype(F32)
    back_b[...] = (lane == row_n).astype(F32).astype(BF16)
    back_c[...] = (lane == row_n + N).astype(F32).astype(BF16)
    k_row, col_n = iota((LANES, GN), 0), iota((LANES, GN), 1) % N
    sel_b[...] = ((k_row == col_n) | (k_row == col_n + 2 * N)).astype(F32).astype(BF16)
    sel_c[...] = ((k_row == col_n + N) | (k_row == col_n + 3 * N)).astype(F32).astype(BF16)
    dmask[...] = (iota((GROUP, GN), 1) // N == iota((GROUP, GN), 0)).astype(F32)
    xwp[: R + 2 * N, :] = xw_ref[...]
    xwp[R + 2 * N :, :] = jnp.zeros((LANES - 2 * N, C), BF16)

    xpad[:8, :] = jnp.zeros((8, C), F32)
    xpad[8:, :] = x_ref[...].astype(F32)
    cw = cw_ref[...]

    def conv(first, count):
        total = jnp.broadcast_to(cb_ref[...], (count, C))
        for k in range(4):
            total = total + cw[k : k + 1] * xpad[first + 5 + k : first + 5 + k + count, :]
        return total

    pre_act[...] = conv(0, T)
    pl.semaphore_wait(barrier, NC + NS - 2)
    halo = Exchange("seq", NS, ms, s_h, r_h)

    def halo_copy(src, dst, k, peer):
        return pltpu.make_async_remote_copy(
            src_ref=src, dst_ref=dst, send_sem=s_h.at[k], recv_sem=r_h.at[k],
            device_id={"seq": peer}, device_id_type=MESH,
        )

    after, before = lax.rem(ms + 1, NS), lax.rem(ms + NS - 1, NS)

    @pl.when(ms < NS - 1)
    def _():
        halo_copy(x_ref.at[T - 16 :, :], halo_x, 0, after).start()

    gate = z_ref[...].astype(F32)
    cot = g_ref[...].astype(F32)
    sig = jax.nn.sigmoid(gate)
    gy[...] = cot * gate * sig
    gz[...] = cot * sig * (1.0 + gate * (1.0 - sig))

    @pl.when(ms > 0)
    def _():
        halo_copy(halo_x, halo_x, 0, before).wait_recv()
        xpad[:8, :] = halo_x[...].astype(F32)[8:16]
        pre_act[:8, :] = conv(0, 8)

    act = pre_act[...]
    u_bf[...] = (act * jax.nn.sigmoid(act)).astype(BF16)

    part[...] = dot_nt(u_bf[...], xwp[...])
    send1[...] = part[...].astype(BF16)

    def my_rows(ref):
        return ref[pl.ds(pl.multiple_of(mc * ROWS, ROWS), ROWS), :]

    def block(ref, i, size):
        return ref.at[pl.ds(pl.multiple_of(i * size, size), size), :]

    def scatter(ex, src, slots, size):
        for peer in ex.peers():
            ex.send(block(src, peer, size), slots.at[ex.me], peer)

    def collect(ex, slots, own):
        for peer in ex.peers():
            ex.wait_recv(slots.at[peer], peer)
        for peer in ex.peers():
            own = own + slots[peer].astype(F32)
        return own

    def spread(ex, buf, size):
        for peer in ex.peers():
            ex.send(block(buf, ex.me, size), block(buf, ex.me, size), peer)

    def arrive(ex, buf, size):
        for peer in ex.peers():
            ex.wait_recv(block(buf, peer, size), peer)

    scatter(chan(0), send1, rs1, ROWS)
    rate = -jnp.exp(al_ref[...])
    rate2 = rate * LOG2E
    proj = collect(chan(0), rs1, my_rows(part))
    low = proj[:, :R]
    inv = lax.rsqrt(jnp.mean(low * low, -1, keepdims=True) + EPS)
    low_own[...] = low
    inv_own[...] = jnp.broadcast_to(inv, inv_own.shape)
    tail = proj[:, R:]
    tail_hi = tail.astype(BF16).astype(F32)
    tail = tail_hi + pltpu.roll(tail - tail_hi, 2 * N, 1)
    mine = pl.ds(pl.multiple_of(mc * ROWS, ROWS), ROWS)
    ag1[mine, :R] = (low * inv * dg_ref[...]).astype(BF16)
    ag1[mine, R:] = tail.astype(BF16)
    spread(chan(1), ag1, ROWS)
    arrive(chan(1), ag1, ROWS)

    soft = dot(ag1[:, :R], dw_ref[...]) + db_ref[...]
    pre_soft[...] = soft
    step = softplus(soft)
    delta[...] = step
    drive[...] = step * u_bf[...].astype(F32)
    tot[...] = jnp.sum(step, 0, keepdims=True)
    for peer in states(2).peers():
        states(2).send(tot, in_tot.at[ms], peer)

    ones = jnp.ones((LANES, LANES), BF16)

    def widen(i, carry):
        rows = ag1[pl.ds(pl.multiple_of(i * GROUP, GROUP), GROUP), R:]
        spread_rows = dot(e_exp[...], rows)
        at = pl.ds(pl.multiple_of(i * GN, GN), GN)
        bB[at, :] = dot((spread_rows * m_b[...]).astype(BF16), ones)
        cB[at, :] = dot((spread_rows * m_c[...]).astype(BF16), ones)
        return carry

    lax.fori_loop(0, NB, widen, 0)

    def row(ref, t):
        return ref[pl.ds(t, 1), :]

    def state_at(t):
        return pl.ds(pl.multiple_of(t * N, N), N)

    def wide(ref, t):
        return jnp.concatenate([ref[state_at(t), :]] * (C // LANES), axis=1)

    zero_state = jnp.zeros((N, C), F32)

    def forward_part(i, h):
        for j in range(GROUP):
            t = i * GROUP + j
            a = jnp.exp2(row(delta, t) * rate2)
            a_buf[state_at(t), :] = a
            h = a * h + row(drive, t) * wide(bB, t)
        return h

    st_f[...] = lax.fori_loop(0, NB, forward_part, zero_state).astype(BF16)
    for d in range(1, NS):

        @pl.when(ms + d < NS)
        def _(d=d):
            states(0).send(st_f, in_f.at[ms], ms + d)

    def backward_part(i, g):
        for j in range(GROUP):
            t = T - 1 - (i * GROUP + j)
            g = a_buf[state_at(t), :] * (row(gy, t) * wide(cB, t) + g)
        return g

    st_b[...] = lax.fori_loop(0, NB, backward_part, zero_state).astype(BF16)
    for d in range(1, NS):

        @pl.when(ms - d >= 0)
        def _(d=d):
            states(1).send(st_b, in_b.at[ms], ms - d)

    for peer in states(2).peers():
        states(2).wait_recv(in_tot.at[peer], peer)
    carry_f[...] = zero_state
    for s in range(NS - 1):

        @pl.when(s < ms)
        def _(s=s):
            states(0).wait_recv(in_f.at[s], s)
            carry_f[...] = jnp.exp2(in_tot[s] * rate2) * carry_f[...] + in_f[s].astype(F32)

    start = carry_f[...]
    h_buf[:N, :] = start.astype(BF16)

    def forward(i, h):
        for j in range(GROUP):
            t = i * GROUP + j
            h = a_buf[state_at(t), :] * h + row(drive, t) * wide(bB, t)
            h_buf[state_at(t + 1), :] = h.astype(BF16)
        return h

    lax.fori_loop(0, NB, forward, start)

    def tokens(i):
        return pl.ds(pl.multiple_of(i * GROUP, GROUP), GROUP)

    def after_forward(i, carry):
        coef = ag1[tokens(i), R:]
        h_rows = h_buf[pl.ds(pl.multiple_of(i * GN + N, N), GN), :]
        c_diag = (dot(coef, sel_c[...]) * dmask[...]).astype(BF16)
        yv[tokens(i), :] = dot(c_diag, h_rows)
        c_all = dot_nt(gy[tokens(i), :].astype(BF16), h_rows) * dmask[...]
        bcg[tokens(i), :] = dot(c_all.astype(BF16), back_c[...])
        return carry

    lax.fori_loop(0, NB, after_forward, 0)

    carry_b[...] = zero_state
    for s in range(NS - 1, 0, -1):

        @pl.when(s > ms)
        def _(s=s):
            states(1).wait_recv(in_b.at[s], s)
            carry_b[...] = jnp.exp2(in_tot[s] * rate2) * carry_b[...] + in_b[s].astype(F32)

    def backward(i, carry):
        g, acc = carry
        for j in range(GROUP):
            t = T - 1 - (i * GROUP + j)
            lam = row(gy, t) * wide(cB, t) + g
            g = a_buf[state_at(t), :] * lam
            hold = g * h_buf[state_at(t), :].astype(F32)
            acc = acc + hold * row(delta, t)
            lam_buf[state_at(t), :] = lam.astype(BF16)
            ha_buf[state_at(t), :] = (hold * rate).astype(BF16)
        return g, acc

    _, rate_sum = lax.fori_loop(0, NB, backward, (carry_b[...], zero_state))

    def after_backward(i, carry):
        coef = ag1[tokens(i), R:]
        at = pl.ds(pl.multiple_of(i * GN, GN), GN)
        lam_rows = lam_buf[at, :]
        b_diag = (dot(coef, sel_b[...]) * dmask[...]).astype(BF16)
        adj_b = dot(b_diag, lam_rows)
        by_rate = dot(dmask[...].astype(BF16), ha_buf[at, :])
        b_all = dot_nt(drive[tokens(i), :].astype(BF16), lam_rows) * dmask[...]
        bcg[tokens(i), :] = bcg[tokens(i), :] + dot(b_all.astype(BF16), back_b[...])
        pre = (by_rate + adj_b * u_bf[tokens(i), :].astype(F32)) * jax.nn.sigmoid(pre_soft[tokens(i), :])
        pregrad[tokens(i), :] = pre
        prehalf[tokens(i), :] = pre.astype(BF16)
        uscan[tokens(i), :] = ds_ref[...] * gy[tokens(i), :] + delta[tokens(i), :] * adj_b
        return carry

    lax.fori_loop(0, NB, after_backward, 0)

    part[:, :R] = dot_nt(prehalf[...], dw_ref[...])
    part[:, R:] = bcg[...]
    send2[...] = part[...].astype(BF16)
    scatter(chan(2), send2, rs2, ROWS)

    dw_f[...] = dot_tn(ag1[:, :R], prehalf[...])
    dw_send[...] = dw_f[...].astype(BF16)
    scatter(seq(0), dw_send, dw_rs, RB)
    u32 = u_bf[...].astype(F32)
    zg_o[...] = (gz[...] * (yv[...] + ds_ref[...] * u32)).astype(BF16)
    sm_f[...] = jnp.zeros_like(sm_f)
    sm_f[2 * N : 3 * N, :] = rate_sum * rate
    sm_f[3 * N + 5 : 3 * N + 6, :] = jnp.sum(pregrad[...], 0, keepdims=True)
    sm_f[3 * N + 6 : 3 * N + 7, :] = jnp.sum(gy[...] * u32, 0, keepdims=True)

    grad_rows = collect(chan(2), rs2, my_rows(part))
    low = low_own[...]
    inv = inv_own[:, :1]
    scaled = grad_rows[:, :R] * dg_ref[...]
    low_grad = inv * scaled - low * (inv * inv * inv) * jnp.mean(scaled * low, -1, keepdims=True)
    gain = jnp.sum(grad_rows[:, :R] * low * inv, 0, keepdims=True)
    half = LANES // 2
    lanes = iota((ROWS, LANES), 1)
    rows = iota((ROWS, LANES), 0)
    g0 = jnp.broadcast_to(gain[:, :LANES], (ROWS, LANES))
    g1 = jnp.broadcast_to(gain[:, LANES:], (ROWS, LANES))
    q = rows % 4
    gq = jnp.where(q == 0, pltpu.roll(g0, half, 1), jnp.where(q == 1, g0, jnp.where(q == 2, pltpu.roll(g1, half, 1), g1)))
    g_hi = gq.astype(BF16).astype(F32)
    g_rows = jnp.where(rows < 4, g_hi, jnp.where(rows < 8, gq - g_hi, 0.0))
    ag2[mine, :R] = low_grad.astype(BF16)
    ag2[mine, R:] = jnp.where(lanes < half, grad_rows[:, R:], g_rows).astype(BF16)
    spread(chan(3), ag2, ROWS)

    own = collect(seq(0), dw_rs, dw_f[pl.ds(pl.multiple_of(ms * RB, RB), RB), :])
    dw_ag[pl.ds(pl.multiple_of(ms * RB, RB), RB), :] = own.astype(BF16)
    spread(seq(1), dw_ag, RB)

    arrive(chan(3), ag2, ROWS)
    keep = iota((T, W), 1) < R + 2 * N
    pg = jnp.where(keep, ag2[...].astype(F32), 0.0).astype(BF16)
    act = pre_act[...]
    total = uscan[...] + dot(pg, xwp[...])
    act_grad = total * silu_grad(act)
    apad[:T, :] = act_grad
    apad[T:, :] = jnp.zeros((8, C), F32)

    @pl.when(ms > 0)
    def _():
        halo_copy(apad.at[:8, :], halo_a, 1, before).start()

    xl_f[...] = dot_tn(pg, u_bf[...])
    xl_send[...] = xl_f[:R, :].astype(BF16)
    scatter(seq(2), xl_send, xl_rs, RB)
    sm_f[: 2 * N, :] = xl_f[R : R + 2 * N, :]
    for k in range(4):
        sm_f[3 * N + k : 3 * N + k + 1, :] = jnp.sum(act_grad * xpad[5 + k : 5 + k + T, :], 0, keepdims=True)
    sm_f[3 * N + 4 : 3 * N + 5, :] = jnp.sum(act_grad, 0, keepdims=True)
    g_sum = jnp.zeros((ROWS, LANES), F32)
    for c in range(NC):
        g_sum = g_sum + ag2[c * ROWS : (c + 1) * ROWS, R:].astype(F32)
    gq = g_sum[:4] + g_sum[4:8]
    low_half = iota((1, LANES), 1) < half
    for k in range(2):
        sm_f[3 * N + 7 : 3 * N + 8, k * LANES : (k + 1) * LANES] = jnp.where(
            low_half, pltpu.roll(gq[2 * k : 2 * k + 1], half, 1), gq[2 * k + 1 : 2 * k + 2]
        )
    scatter(seq(3), sm_f, sm_rs, SB)

    @pl.when(ms < NS - 1)
    def _():
        halo_copy(halo_a, halo_a, 1, after).wait_recv()
        apad[T:, :] = halo_a[...]

    total = jnp.zeros((T, C), F32)
    for k in range(4):
        total = total + cw[k : k + 1] * apad[3 - k : 3 - k + T, :]
    xg_o[...] = total.astype(BF16)

    at = pl.ds(pl.multiple_of(ms * RB, RB), RB)
    xl_ag[at, :] = collect(seq(2), xl_rs, xl_f[at, :]).astype(BF16)
    spread(seq(4), xl_ag, RB)
    at = pl.ds(pl.multiple_of(ms * SB, SB), SB)
    sm_ag[at, :] = collect(seq(3), sm_rs, sm_f[at, :])
    spread(seq(5), sm_ag, SB)
    arrive(seq(1), dw_ag, RB)
    arrive(seq(4), xl_ag, RB)
    arrive(seq(5), sm_ag, SB)

    for k, size, src in ((0, ROWS, send1), (1, ROWS, ag1), (2, ROWS, send2), (3, ROWS, ag2)):
        for peer in chan(k).peers():
            chan(k).wait_send(src.at[:size, :], peer)
    for k, size, src in ((0, RB, dw_send), (1, RB, dw_ag), (2, RB, xl_send), (3, SB, sm_f), (4, RB, xl_ag), (5, SB, sm_ag)):
        for peer in seq(k).peers():
            seq(k).wait_send(src.at[:size, :], peer)
    for peer in states(2).peers():
        states(2).wait_send(tot, peer)
    for d in range(1, NS):

        @pl.when(ms + d < NS)
        def _(d=d):
            states(0).wait_send(st_f, ms + d)

        @pl.when(ms - d >= 0)
        def _(d=d):
            states(1).wait_send(st_b, ms - d)

    @pl.when(ms < NS - 1)
    def _():
        halo_copy(halo_x, halo_x, 0, after).wait_send()

    @pl.when(ms > 0)
    def _():
        halo_copy(halo_a, halo_a, 1, before).wait_send()


def finish_kernel(dims, xg, zg, dw_sum, xl_sum, sm_sum, xg_o, zg_o, cwg_o, cbg_o, xpg_o, dwg_o, dbg_o, alg_o, dsg_o, dgg_o):
    T, C, NS, NC, R, N = dims
    scale = 1.0 / math.sqrt(T * NS)
    xg_o[...] = xg[...]
    zg_o[...] = zg[...]
    dwg_o[...] = scale * dw_sum[...].astype(F32)
    xpg_o[:R, :] = scale * xl_sum[...].astype(F32)
    xpg_o[R:, :] = scale * sm_sum[: 2 * N, :]
    alg_o[...] = scale * sm_sum[2 * N : 3 * N, :]
    cwg_o[...] = scale * sm_sum[3 * N : 3 * N + 4, :]
    cbg_o[...] = scale * sm_sum[3 * N + 4 : 3 * N + 5, :]
    dbg_o[...] = scale * sm_sum[3 * N + 5 : 3 * N + 6, :]
    dsg_o[...] = scale * sm_sum[3 * N + 6 : 3 * N + 7, :]
    dgg_o[...] = scale * sm_sum[3 * N + 7 : 3 * N + 8, :R]


def per_device(counts, x_in, z_in, grad_out, conv_w, conv_b, xproj_w, dt_w, dt_bias, a_log, d_skip, dt_gain):
    T, C = x_in.shape
    R = dt_w.shape[0]
    N = a_log.shape[1]
    NS, NC = counts
    ROWS = T // NC
    W = R + LANES
    GN = GROUP * N
    SM = 4 * N
    dims = (T, C, NS, NC, R, N)

    def f32(*shape):
        return pltpu.VMEM(shape, F32)

    def b16(*shape):
        return pltpu.VMEM(shape, BF16)

    dma = pltpu.SemaphoreType.DMA
    scratch = dict(
        xpad=f32(T + 8, C), pre_act=f32(T, C), u_bf=b16(T, C), gy=f32(T, C), gz=f32(T, C),
        xwp=b16(W, C), part=f32(T, W), send1=b16(T, W), rs1=b16(NC, ROWS, W), ag1=b16(T, W),
        low_own=f32(ROWS, R), inv_own=f32(ROWS, LANES),
        pre_soft=f32(T, C), delta=f32(T, C), drive=f32(T, C), bB=f32(T * N, LANES), cB=f32(T * N, LANES),
        a_buf=f32(T * N, C), h_buf=b16((T + 1) * N, C), lam_buf=b16(T * N, C), ha_buf=b16(T * N, C),
        st_f=b16(N, C), st_b=b16(N, C), tot=f32(1, C), in_f=b16(NS, N, C), in_b=b16(NS, N, C),
        in_tot=f32(NS, 1, C), carry_f=f32(N, C), carry_b=f32(N, C),
        e_exp=b16(GN, GROUP), m_b=f32(GN, LANES), m_c=f32(GN, LANES), sel_b=b16(LANES, GN), sel_c=b16(LANES, GN),
        dmask=f32(GROUP, GN), back_b=b16(GN, LANES), back_c=b16(GN, LANES),
        yv=f32(T, C), bcg=f32(T, LANES), uscan=f32(T, C), pregrad=f32(T, C), prehalf=b16(T, C),
        send2=b16(T, W), rs2=b16(NC, ROWS, W), ag2=b16(T, W),
        dw_f=f32(R, C), dw_send=b16(R, C), dw_rs=b16(NS, R // NS, C),
        xl_f=f32(W, C), xl_send=b16(R, C), xl_rs=b16(NS, R // NS, C),
        sm_f=f32(SM, C), sm_rs=f32(NS, SM // NS, C),
        halo_x=b16(16, C), halo_a=f32(8, C), apad=f32(T + 8, C),
        s_c=dma((4, NC)), r_c=dma((4, NC)), s_st=dma((3, NS)), r_st=dma((3, NS)),
        s_sq=dma((6, NS)), r_sq=dma((6, NS)), s_h=dma((2,)), r_h=dma((2,)),
    )
    S = jax.ShapeDtypeStruct
    vmem = pl.BlockSpec(memory_space=pltpu.VMEM)
    raw = pl.pallas_call(
        functools.partial(layer_kernel, dims),
        out_shape=(S((T, C), BF16), S((T, C), BF16), S((R, C), BF16), S((R, C), BF16), S((SM, C), F32)),
        in_specs=[vmem] * 11,
        out_specs=(vmem,) * 5,
        scratch_shapes=list(scratch.values()),
        compiler_params=pltpu.CompilerParams(
            collective_id=0, has_side_effects=True, vmem_limit_bytes=VMEM_BYTES
        ),
    )(
        x_in, z_in, grad_out, conv_w, conv_b[None], xproj_w.T, dt_w, dt_bias[None], a_log.T, d_skip[None], dt_gain[None],
    )
    xg, zg, cwg, cbg, xpg, dwg, dbg, alg, dsg, dgg = pl.pallas_call(
        functools.partial(finish_kernel, dims),
        out_shape=(
            S((T, C), BF16), S((T, C), BF16), S((4, C), F32), S((1, C), F32), S((R + 2 * N, C), F32),
            S((R, C), F32), S((1, C), F32), S((N, C), F32), S((1, C), F32), S((1, R), F32),
        ),
        in_specs=[vmem] * 5,
        out_specs=(vmem,) * 10,
        compiler_params=pltpu.CompilerParams(vmem_limit_bytes=VMEM_BYTES),
    )(*raw)
    return xg, zg, cwg, cbg[0], xpg.T, dwg, dbg[0], alg.T, dsg[0], dgg[0]


def solution(mesh):
    placed = (
        P("seq", "chan"),
        P("seq", "chan"),
        P("seq", "chan"),
        P(None, "chan"),
        P("chan"),
        P("chan", None),
        P(None, "chan"),
        P("chan"),
        P("chan", None),
        P("chan"),
        P(),
    )
    counts = (mesh.shape["seq"], mesh.shape["chan"])
    return jax.shard_map(
        functools.partial(per_device, counts),
        mesh=mesh,
        in_specs=placed,
        out_specs=(
            P("seq", "chan"),
            P("seq", "chan"),
            P(None, "chan"),
            P("chan"),
            P("chan", None),
            P(None, "chan"),
            P("chan"),
            P("chan", None),
            P("chan"),
            P(),
        ),
        check_vma=False,
    )
```

```python
import functools
import math

import jax
import jax.numpy as jnp
from jax import lax
from jax.experimental import pallas as pl
from jax.experimental.pallas import tpu as pltpu
from jax.sharding import PartitionSpec as P

EPS = 1e-06
LOG2E = 1.4426950408889634
LANES = 128
GROUP = 16
F32 = jnp.float32
BF16 = jnp.bfloat16
MESH = pl.DeviceIdType.MESH
VMEM_BYTES = 60 * 1024 * 1024
CHUNK = 4
UNROLL_FP = UNROLL_BP = UNROLL_F = UNROLL_B = 16


def dot(a, b):
    return jnp.dot(a, b, preferred_element_type=F32)


def dot_nt(a, b):
    return lax.dot_general(a, b, (((1,), (1,)), ((), ())), preferred_element_type=F32)


def dot_tn(a, b):
    return lax.dot_general(a, b, (((0,), (0,)), ((), ())), preferred_element_type=F32)


def iota(shape, dim):
    return lax.broadcasted_iota(jnp.int32, shape, dim)


def silu_grad(value):
    sigma = jax.nn.sigmoid(value)
    return sigma * (1.0 + value * (1.0 - sigma))


def softplus(value):
    return jnp.maximum(value, 0.0) + jnp.log1p(jnp.exp(-jnp.abs(value)))


class Exchange:
    def __init__(self, axis, count, me, send_sem, recv_sem):
        self.axis, self.count, self.me = axis, count, me
        self.send_sem, self.recv_sem = send_sem, recv_sem

    def _copy(self, src, dst, send, recv, peer):
        return pltpu.make_async_remote_copy(
            src_ref=src,
            dst_ref=dst,
            send_sem=self.send_sem.at[send],
            recv_sem=self.recv_sem.at[recv],
            device_id={self.axis: peer},
            device_id_type=MESH,
        )

    def peers(self):
        return [lax.rem(self.me + d, self.count) for d in range(1, self.count)]

    def send(self, src, dst, peer):
        self._copy(src, dst, peer, self.me, peer).start()

    def wait_recv(self, slot, peer):
        self._copy(slot, slot, peer, peer, peer).wait_recv()

    def wait_send(self, slot, peer):
        self._copy(slot, slot, peer, peer, peer).wait_send()


def layer_kernel(dims, *refs):
    T, C, NS, NC, R, N = dims
    hbm, refs = refs[:11], refs[11:]
    (xg_o, zg_o, dw_ag, xl_ag, sm_ag,
     x_ref, z_ref, g_ref, cw_ref, cb_ref, xw_ref, dw_ref, db_ref, al_ref, ds_ref, dg_ref,
     xpad, pre_act, act_slope, u_bf, gy, gz, part, send1, rs1, ag1, low_own, inv_own,
     pre_soft, delta, drive, bB, cB, a_buf, h_buf, lam_buf, ha_buf,
     st_f, st_b, tot, in_f, in_b, in_tot, carry_f, carry_b,
     e_exp, m_b, m_c, sel_b, sel_c, dmask, back_b, back_c,
     bcg, uscan, pregrad, prehalf, send2, rs2, ag2,
     dw_f, dw_send, dw_rs, xl_f, xl_send, xl_rs, sm_f, sm_rs,
     halo_x, halo_a, apad,
     s_in, s_c, r_c, s_st, r_st, s_sq, r_sq, s_h, r_h) = refs
    ROWS = T // NC
    W = R + LANES
    P2 = R + 2 * N
    NB = T // GROUP
    GN = GROUP * N
    RB = R // NS
    SM = sm_f.shape[0]
    SB = SM // NS
    ms, mc = lax.axis_index("seq"), lax.axis_index("chan")

    def chan(k):
        return Exchange("chan", NC, mc, s_c.at[k], r_c.at[k])

    def seq(k):
        return Exchange("seq", NS, ms, s_sq.at[k], r_sq.at[k])

    def states(k):
        return Exchange("seq", NS, ms, s_st.at[k], r_st.at[k])

    barrier = pltpu.get_barrier_semaphore()
    for d in range(1, NC):
        pl.semaphore_signal(barrier, inc=1, device_id={"chan": lax.rem(mc + d, NC)}, device_id_type=MESH)
    for d in range(1, NS):
        pl.semaphore_signal(barrier, inc=1, device_id={"seq": lax.rem(ms + d, NS)}, device_id_type=MESH)
    local = (x_ref, z_ref, g_ref, cw_ref, cb_ref, xw_ref, dw_ref, db_ref, al_ref, ds_ref, dg_ref)
    fetch = [pltpu.make_async_copy(hbm[k], local[k], s_in.at[k]) for k in range(11)]
    for k in (0, 3, 4, 5, 1, 2, 6, 7, 8, 9, 10):
        fetch[k].start()

    xpad[:8, :] = jnp.zeros((8, C), F32)
    for k in (0, 3, 4):
        fetch[k].wait()
    xpad[8:, :] = x_ref[...].astype(F32)
    cw = cw_ref[...]

    def conv(first, count):
        total = jnp.broadcast_to(cb_ref[...], (count, C))
        for k in range(4):
            total = total + cw[k : k + 1] * xpad[first + 5 + k : first + 5 + k + count, :]
        pre_act[first : first + count, :] = total
        u_bf[first : first + count, :] = (total * jax.nn.sigmoid(total)).astype(BF16)

    def project(first, count):
        sums = dot_nt(u_bf[first : first + count, :], xw_ref[...])
        part[first : first + count, :R] = sums[:, :R]
        part[first : first + count, R:P2] = sums[:, R:P2]
        send1[first : first + count, :R] = sums[:, :R].astype(BF16)
        send1[first : first + count, R:P2] = sums[:, R:P2].astype(BF16)

    def halo_copy(src, dst, k, peer):
        return pltpu.make_async_remote_copy(
            src_ref=src, dst_ref=dst, send_sem=s_h.at[k], recv_sem=r_h.at[k],
            device_id={"seq": peer}, device_id_type=MESH,
        )

    def block(ref, i, size):
        return ref.at[pl.ds(pl.multiple_of(i * size, size), size), :]

    def scatter(ex, src, slots, size):
        for peer in ex.peers():
            ex.send(block(src, peer, size), slots.at[ex.me], peer)

    def collect(ex, slots, own):
        for peer in ex.peers():
            ex.wait_recv(slots.at[peer], peer)
        for peer in ex.peers():
            own = own + slots[peer].astype(F32)
        return own

    def spread(ex, buf, size):
        for peer in ex.peers():
            ex.send(block(buf, ex.me, size), block(buf, ex.me, size), peer)

    def arrive(ex, buf, size):
        for peer in ex.peers():
            ex.wait_recv(block(buf, peer, size), peer)

    after, before = lax.rem(ms + 1, NS), lax.rem(ms + NS - 1, NS)
    pl.semaphore_wait(barrier, NC + NS - 2)

    @pl.when(ms < NS - 1)
    def _():
        halo_copy(x_ref.at[T - 16 :, :], halo_x, 0, after).start()

    part[:, R:] = jnp.zeros((T, LANES), F32)
    send1[:, R:] = jnp.zeros((T, LANES), BF16)
    conv(0, T)
    fetch[5].wait()
    project(ROWS, T - ROWS)
    for peer in chan(0).peers():

        @pl.when(peer != 0)
        def _(peer=peer):
            chan(0).send(block(send1, peer, ROWS), rs1.at[mc], peer)

    @pl.when(ms > 0)
    def _():
        halo_copy(halo_x, halo_x, 0, before).wait_recv()
        xpad[:8, :] = halo_x[...].astype(F32)[8:16]
        conv(0, 16)

    project(0, ROWS)

    @pl.when(mc != 0)
    def _():
        chan(0).send(block(send1, 0, ROWS), rs1.at[mc], 0)

    for k in (1, 2, 6, 7, 8, 9, 10):
        fetch[k].wait()
    gate = z_ref[...].astype(F32)
    cot = g_ref[...].astype(F32)
    sig = jax.nn.sigmoid(gate)
    gy[...] = cot * gate * sig
    gz[...] = cot * sig * (1.0 + gate * (1.0 - sig))
    e_exp[...] = (iota((GN, GROUP), 0) // N == iota((GN, GROUP), 1)).astype(F32).astype(BF16)
    row_n, lane = iota((GN, LANES), 0) % N, iota((GN, LANES), 1)
    m_b[...] = ((lane == row_n) | (lane == row_n + 2 * N)).astype(F32)
    m_c[...] = ((lane == row_n + N) | (lane == row_n + 3 * N)).astype(F32)
    back_b[...] = (lane == row_n).astype(F32).astype(BF16)
    back_c[...] = (lane == row_n + N).astype(F32).astype(BF16)
    k_row, col_n = iota((LANES, GN), 0), iota((LANES, GN), 1) % N
    sel_b[...] = ((k_row == col_n) | (k_row == col_n + 2 * N)).astype(F32).astype(BF16)
    sel_c[...] = ((k_row == col_n + N) | (k_row == col_n + 3 * N)).astype(F32).astype(BF16)
    dmask[...] = (iota((GROUP, GN), 1) // N == iota((GROUP, GN), 0)).astype(F32)
    rate = -jnp.exp(al_ref[...])
    rate2 = rate * LOG2E

    def my_rows(ref):
        return ref[pl.ds(pl.multiple_of(mc * ROWS, ROWS), ROWS), :]

    proj = collect(chan(0), rs1, my_rows(part))
    low = proj[:, :R]
    inv = lax.rsqrt(jnp.mean(low * low, -1, keepdims=True) + EPS)
    low_own[...] = low
    inv_own[...] = jnp.broadcast_to(inv, inv_own.shape)
    tail = proj[:, R:]
    tail_hi = tail.astype(BF16).astype(F32)
    tail = tail_hi + pltpu.roll(tail - tail_hi, 2 * N, 1)
    mine = pl.ds(pl.multiple_of(mc * ROWS, ROWS), ROWS)
    ag1[mine, :R] = (low * inv * dg_ref[...]).astype(BF16)
    ag1[mine, R:] = tail.astype(BF16)
    spread(chan(1), ag1, ROWS)
    act_slope[...] = silu_grad(pre_act[...])
    arrive(chan(1), ag1, ROWS)

    soft = dot(ag1[:, :R], dw_ref[...]) + db_ref[...]
    pre_soft[...] = soft
    step = softplus(soft)
    delta[...] = step
    drive[...] = step * u_bf[...].astype(F32)
    tot[...] = jnp.sum(step, 0, keepdims=True)
    for peer in states(2).peers():
        states(2).send(tot, in_tot.at[ms], peer)

    def tokens(i, count=GROUP):
        return pl.ds(pl.multiple_of(i * count, count), count)

    ones = jnp.ones((LANES, LANES), BF16)

    def widen(i, carry):
        spread_rows = [dot(e_exp[...], ag1[tokens(i * CHUNK + k), R:]) for k in range(CHUNK)]
        for k in range(CHUNK):
            at = pl.ds(pl.multiple_of((i * CHUNK + k) * GN, GN), GN)
            bB[at, :] = dot((spread_rows[k] * m_b[...]).astype(BF16), ones)
            cB[at, :] = dot((spread_rows[k] * m_c[...]).astype(BF16), ones)
        return carry

    lax.fori_loop(0, NB // CHUNK, widen, 0)

    def row(ref, t):
        return ref[pl.ds(t, 1), :]

    def state_at(t):
        return pl.ds(pl.multiple_of(t * N, N), N)

    def wide(ref, t):
        return jnp.concatenate([ref[state_at(t), :]] * (C // LANES), axis=1)

    zero_state = jnp.zeros((N, C), F32)

    def forward_part(i, h):
        for j in range(UNROLL_FP):
            t = i * UNROLL_FP + j
            a = jnp.exp2(row(delta, t) * rate2)
            a_buf[state_at(t), :] = a
            h = a * h + row(drive, t) * wide(bB, t)
        return h

    st_f[...] = lax.fori_loop(0, T // UNROLL_FP, forward_part, zero_state).astype(BF16)
    for d in range(1, NS):

        @pl.when(ms + d < NS)
        def _(d=d):
            states(0).send(st_f, in_f.at[ms], ms + d)

    def backward_part(i, g):
        for j in range(UNROLL_BP):
            t = T - 1 - (i * UNROLL_BP + j)
            g = a_buf[state_at(t), :] * (row(gy, t) * wide(cB, t) + g)
        return g

    st_b[...] = lax.fori_loop(0, T // UNROLL_BP, backward_part, zero_state).astype(BF16)
    for d in range(1, NS):

        @pl.when(ms - d >= 0)
        def _(d=d):
            states(1).send(st_b, in_b.at[ms], ms - d)

    for peer in states(2).peers():
        states(2).wait_recv(in_tot.at[peer], peer)
    carry_f[...] = zero_state
    for s in range(NS - 1):

        @pl.when(s < ms)
        def _(s=s):
            states(0).wait_recv(in_f.at[s], s)
            carry_f[...] = jnp.exp2(in_tot[s] * rate2) * carry_f[...] + in_f[s].astype(F32)

    start = carry_f[...]
    h_buf[:N, :] = start.astype(BF16)

    def forward(i, h):
        for j in range(UNROLL_F):
            t = i * UNROLL_F + j
            h = a_buf[state_at(t), :] * h + row(drive, t) * wide(bB, t)
            h_buf[state_at(t + 1), :] = h.astype(BF16)
        return h

    lax.fori_loop(0, T // UNROLL_F, forward, start)

    def state_rows(k):
        return h_buf[pl.ds(pl.multiple_of(k * GN + N, N), GN), :]

    def after_forward(i, carry):
        for k in range(CHUNK):
            k = i * CHUNK + k
            c_all = dot_nt(gy[tokens(k), :].astype(BF16), state_rows(k)) * dmask[...]
            bcg[tokens(k), :] = dot(c_all.astype(BF16), back_c[...])
        return carry

    lax.fori_loop(0, NB // CHUNK, after_forward, 0)

    carry_b[...] = zero_state
    for s in range(NS - 1, 0, -1):

        @pl.when(s > ms)
        def _(s=s):
            states(1).wait_recv(in_b.at[s], s)
            carry_b[...] = jnp.exp2(in_tot[s] * rate2) * carry_b[...] + in_b[s].astype(F32)

    CT = CHUNK * GROUP

    def backward_chunk(i, g):
        c = NB // CHUNK - 1 - i

        def backward(m, g):
            for j in range(UNROLL_B):
                t = c * CT + CT - 1 - (m * UNROLL_B + j)
                lam = row(gy, t) * wide(cB, t) + g
                g = a_buf[state_at(t), :] * lam
                hold = g * h_buf[state_at(t), :].astype(F32)
                lam_buf[state_at(t), :] = lam.astype(BF16)
                ha_buf[state_at(t), :] = (hold * rate).astype(BF16)
            return g

        g = lax.fori_loop(0, CT // UNROLL_B, backward, g)
        at = tokens(c, CT)
        adj_b, by_rate, b_grad = [], [], []
        for k in range(CHUNK):
            k = c * CHUNK + k
            states_k = pl.ds(pl.multiple_of(k * GN, GN), GN)
            lam_rows = lam_buf[states_k, :]
            b_diag = (dot(ag1[tokens(k), R:], sel_b[...]) * dmask[...]).astype(BF16)
            adj_b.append(dot(b_diag, lam_rows))
            by_rate.append(dot(dmask[...].astype(BF16), ha_buf[states_k, :]))
            b_all = dot_nt(drive[tokens(k), :].astype(BF16), lam_rows) * dmask[...]
            b_grad.append(dot(b_all.astype(BF16), back_b[...]))
        adj_b = jnp.concatenate(adj_b, 0)
        pre = (jnp.concatenate(by_rate, 0) + adj_b * u_bf[at, :].astype(F32)) * jax.nn.sigmoid(pre_soft[at, :])
        pregrad[at, :] = pre
        half = pre.astype(BF16)
        prehalf[at, :] = half
        uscan[at, :] = ds_ref[...] * gy[at, :] + delta[at, :] * adj_b
        normed = dot_nt(half, dw_ref[...])
        tail = bcg[at, :] + jnp.concatenate(b_grad, 0)
        part[at, :R] = normed
        part[at, R:] = tail
        send2[at, :R] = normed.astype(BF16)
        send2[at, R:] = tail.astype(BF16)
        for k in range(CHUNK):
            owner = c * CHUNK + k

            @pl.when(owner != mc)
            def _(owner=owner):
                chan(2).send(block(send2, owner, ROWS), rs2.at[mc], owner)

        return g

    lax.fori_loop(0, NB // CHUNK, backward_chunk, carry_b[...])

    dw_f[...] = dot_tn(ag1[:, :R], prehalf[...])
    dw_send[...] = dw_f[...].astype(BF16)
    scatter(seq(0), dw_send, dw_rs, RB)

    def outputs(i, carry):
        y = []
        for k in range(CHUNK):
            k = i * CHUNK + k
            c_diag = (dot(ag1[tokens(k), R:], sel_c[...]) * dmask[...]).astype(BF16)
            y.append(dot(c_diag, state_rows(k)))
        at = tokens(i, CT)
        y = jnp.concatenate(y, 0) + ds_ref[...] * u_bf[at, :].astype(F32)
        zg_o[at, :] = (gz[at, :] * y).astype(BF16)
        return carry

    lax.fori_loop(0, NB // CHUNK, outputs, 0)

    def rate_part(i, acc):
        for j in range(UNROLL_F):
            t = i * UNROLL_F + j
            acc = acc + row(delta, t) * ha_buf[state_at(t), :].astype(F32)
        return acc

    sm_f[2 * N : 3 * N, :] = lax.fori_loop(0, T // UNROLL_F, rate_part, zero_state)
    sm_f[3 * N :, :] = jnp.zeros((SM - 3 * N, C), F32)
    sm_f[3 * N + 5 : 3 * N + 6, :] = jnp.sum(pregrad[...], 0, keepdims=True)
    sm_f[3 * N + 6 : 3 * N + 7, :] = jnp.sum(gy[...] * u_bf[...].astype(F32), 0, keepdims=True)

    grad_rows = collect(chan(2), rs2, my_rows(part))
    low = low_own[...]
    inv = inv_own[:, :1]
    scaled = grad_rows[:, :R] * dg_ref[...]
    low_grad = inv * scaled - low * (inv * inv * inv) * jnp.mean(scaled * low, -1, keepdims=True)
    gain = jnp.sum(grad_rows[:, :R] * low * inv, 0, keepdims=True)
    half = LANES // 2
    lanes = iota((ROWS, LANES), 1)
    rows = iota((ROWS, LANES), 0)
    g0 = jnp.broadcast_to(gain[:, :LANES], (ROWS, LANES))
    g1 = jnp.broadcast_to(gain[:, LANES:], (ROWS, LANES))
    q = rows % 4
    gq = jnp.where(q == 0, pltpu.roll(g0, half, 1), jnp.where(q == 1, g0, jnp.where(q == 2, pltpu.roll(g1, half, 1), g1)))
    g_hi = gq.astype(BF16).astype(F32)
    g_rows = jnp.where(rows < 4, g_hi, jnp.where(rows < 8, gq - g_hi, 0.0))
    ag2[mine, :R] = low_grad.astype(BF16)
    ag2[mine, R:] = jnp.where(lanes < half, grad_rows[:, R:], g_rows).astype(BF16)
    spread(chan(3), ag2, ROWS)

    own = collect(seq(0), dw_rs, dw_f[pl.ds(pl.multiple_of(ms * RB, RB), RB), :])
    dw_ag[pl.ds(pl.multiple_of(ms * RB, RB), RB), :] = own.astype(BF16)
    spread(seq(1), dw_ag, RB)

    arrive(chan(3), ag2, ROWS)

    xl_f[...] = dot_tn(ag2[...], u_bf[...])
    xl_send[...] = xl_f[:R, :].astype(BF16)
    scatter(seq(2), xl_send, xl_rs, RB)
    sm_f[: 2 * N, :] = xl_f[R:P2, :]
    total = uscan[...] + dot(ag2[:, :R], xw_ref[:R, :]) + dot(ag2[:, R:P2], xw_ref[R:, :])
    act_grad = total * act_slope[...]
    apad[:T, :] = act_grad
    apad[T:, :] = jnp.zeros((8, C), F32)

    @pl.when(ms > 0)
    def _():
        halo_copy(apad.at[:8, :], halo_a, 1, before).start()

    for k in range(4):
        sm_f[3 * N + k : 3 * N + k + 1, :] = jnp.sum(act_grad * xpad[5 + k : 5 + k + T, :], 0, keepdims=True)
    sm_f[3 * N + 4 : 3 * N + 5, :] = jnp.sum(act_grad, 0, keepdims=True)
    g_sum = jnp.zeros((ROWS, LANES), F32)
    for c in range(NC):
        g_sum = g_sum + ag2[c * ROWS : (c + 1) * ROWS, R:].astype(F32)
    gq = g_sum[:4] + g_sum[4:8]
    low_half = iota((1, LANES), 1) < half
    for k in range(2):
        sm_f[3 * N + 7 : 3 * N + 8, k * LANES : (k + 1) * LANES] = jnp.where(
            low_half, pltpu.roll(gq[2 * k : 2 * k + 1], half, 1), gq[2 * k + 1 : 2 * k + 2]
        )
    scatter(seq(3), sm_f, sm_rs, SB)

    @pl.when(ms < NS - 1)
    def _():
        halo_copy(halo_a, halo_a, 1, after).wait_recv()
        apad[T:, :] = halo_a[...]

    total = jnp.zeros((T, C), F32)
    for k in range(4):
        total = total + cw[k : k + 1] * apad[3 - k : 3 - k + T, :]
    xg_o[...] = total.astype(BF16)

    at = pl.ds(pl.multiple_of(ms * RB, RB), RB)
    xl_ag[at, :] = collect(seq(2), xl_rs, xl_f[at, :]).astype(BF16)
    spread(seq(4), xl_ag, RB)
    at = pl.ds(pl.multiple_of(ms * SB, SB), SB)
    sm_ag[at, :] = collect(seq(3), sm_rs, sm_f[at, :])
    spread(seq(5), sm_ag, SB)
    arrive(seq(1), dw_ag, RB)
    arrive(seq(4), xl_ag, RB)
    arrive(seq(5), sm_ag, SB)

    for k, size, src in ((0, ROWS, send1), (1, ROWS, ag1), (2, ROWS, send2), (3, ROWS, ag2)):
        for peer in chan(k).peers():
            chan(k).wait_send(src.at[:size, :], peer)
    for k, size, src in ((0, RB, dw_send), (1, RB, dw_ag), (2, RB, xl_send), (3, SB, sm_f), (4, RB, xl_ag), (5, SB, sm_ag)):
        for peer in seq(k).peers():
            seq(k).wait_send(src.at[:size, :], peer)
    for peer in states(2).peers():
        states(2).wait_send(tot, peer)
    for d in range(1, NS):

        @pl.when(ms + d < NS)
        def _(d=d):
            states(0).wait_send(st_f, ms + d)

        @pl.when(ms - d >= 0)
        def _(d=d):
            states(1).wait_send(st_b, ms - d)

    @pl.when(ms < NS - 1)
    def _():
        halo_copy(halo_x, halo_x, 0, after).wait_send()

    @pl.when(ms > 0)
    def _():
        halo_copy(halo_a, halo_a, 1, before).wait_send()


def finish_kernel(dims, xg, zg, dw_sum, xl_sum, sm_sum, xg_o, zg_o, cwg_o, cbg_o, xpg_o, dwg_o, dbg_o, alg_o, dsg_o, dgg_o):
    T, C, NS, NC, R, N = dims
    scale = 1.0 / math.sqrt(T * NS)
    xg_o[...] = xg[...]
    zg_o[...] = zg[...]
    dwg_o[...] = scale * dw_sum[...].astype(F32)
    xpg_o[:R, :] = scale * xl_sum[...].astype(F32)
    xpg_o[R:, :] = scale * sm_sum[: 2 * N, :]
    alg_o[...] = scale * sm_sum[2 * N : 3 * N, :]
    cwg_o[...] = scale * sm_sum[3 * N : 3 * N + 4, :]
    cbg_o[...] = scale * sm_sum[3 * N + 4 : 3 * N + 5, :]
    dbg_o[...] = scale * sm_sum[3 * N + 5 : 3 * N + 6, :]
    dsg_o[...] = scale * sm_sum[3 * N + 6 : 3 * N + 7, :]
    dgg_o[...] = scale * sm_sum[3 * N + 7 : 3 * N + 8, :R]


def per_device(counts, x_in, z_in, grad_out, conv_w, conv_b, xproj_w, dt_w, dt_bias, a_log, d_skip, dt_gain):
    T, C = x_in.shape
    R = dt_w.shape[0]
    N = a_log.shape[1]
    NS, NC = counts
    ROWS = T // NC
    W = R + LANES
    GN = GROUP * N
    SM = 4 * N
    dims = (T, C, NS, NC, R, N)

    def f32(*shape):
        return pltpu.VMEM(shape, F32)

    def b16(*shape):
        return pltpu.VMEM(shape, BF16)

    dma = pltpu.SemaphoreType.DMA
    scratch = dict(
        x_ref=b16(T, C), z_ref=b16(T, C), g_ref=b16(T, C), cw_ref=f32(4, C), cb_ref=f32(1, C), xw_ref=b16(R + 2 * N, C),
        dw_ref=b16(R, C), db_ref=f32(1, C), al_ref=f32(N, C), ds_ref=f32(1, C), dg_ref=f32(1, R),
        xpad=f32(T + 8, C), pre_act=f32(T, C), act_slope=f32(T, C), u_bf=b16(T, C), gy=f32(T, C), gz=f32(T, C),
        part=f32(T, W), send1=b16(T, W), rs1=b16(NC, ROWS, W), ag1=b16(T, W),
        low_own=f32(ROWS, R), inv_own=f32(ROWS, LANES),
        pre_soft=f32(T, C), delta=f32(T, C), drive=f32(T, C), bB=f32(T * N, LANES), cB=f32(T * N, LANES),
        a_buf=f32(T * N, C), h_buf=b16((T + 1) * N, C), lam_buf=b16(T * N, C), ha_buf=b16(T * N, C),
        st_f=b16(N, C), st_b=b16(N, C), tot=f32(1, C), in_f=b16(NS, N, C), in_b=b16(NS, N, C),
        in_tot=f32(NS, 1, C), carry_f=f32(N, C), carry_b=f32(N, C),
        e_exp=b16(GN, GROUP), m_b=f32(GN, LANES), m_c=f32(GN, LANES), sel_b=b16(LANES, GN), sel_c=b16(LANES, GN),
        dmask=f32(GROUP, GN), back_b=b16(GN, LANES), back_c=b16(GN, LANES),
        bcg=f32(T, LANES), uscan=f32(T, C), pregrad=f32(T, C), prehalf=b16(T, C),
        send2=b16(T, W), rs2=b16(NC, ROWS, W), ag2=b16(T, W),
        dw_f=f32(R, C), dw_send=b16(R, C), dw_rs=b16(NS, R // NS, C),
        xl_f=f32(W, C), xl_send=b16(R, C), xl_rs=b16(NS, R // NS, C),
        sm_f=f32(SM, C), sm_rs=f32(NS, SM // NS, C),
        halo_x=b16(16, C), halo_a=f32(8, C), apad=f32(T + 8, C),
        s_in=dma((11,)), s_c=dma((4, NC)), r_c=dma((4, NC)), s_st=dma((3, NS)), r_st=dma((3, NS)),
        s_sq=dma((6, NS)), r_sq=dma((6, NS)), s_h=dma((2,)), r_h=dma((2,)),
    )
    S = jax.ShapeDtypeStruct
    vmem = pl.BlockSpec(memory_space=pltpu.VMEM)
    raw = pl.pallas_call(
        functools.partial(layer_kernel, dims),
        out_shape=(S((T, C), BF16), S((T, C), BF16), S((R, C), BF16), S((R, C), BF16), S((SM, C), F32)),
        in_specs=[pl.BlockSpec(memory_space=pl.ANY)] * 11,
        out_specs=(vmem,) * 5,
        scratch_shapes=list(scratch.values()),
        compiler_params=pltpu.CompilerParams(
            collective_id=0, has_side_effects=True, vmem_limit_bytes=VMEM_BYTES
        ),
    )(
        x_in, z_in, grad_out, conv_w, conv_b[None], xproj_w.T, dt_w, dt_bias[None], a_log.T, d_skip[None], dt_gain[None],
    )
    xg, zg, cwg, cbg, xpg, dwg, dbg, alg, dsg, dgg = pl.pallas_call(
        functools.partial(finish_kernel, dims),
        out_shape=(
            S((T, C), BF16), S((T, C), BF16), S((4, C), F32), S((1, C), F32), S((R + 2 * N, C), F32),
            S((R, C), F32), S((1, C), F32), S((N, C), F32), S((1, C), F32), S((1, R), F32),
        ),
        in_specs=[vmem] * 5,
        out_specs=(vmem,) * 10,
        compiler_params=pltpu.CompilerParams(vmem_limit_bytes=VMEM_BYTES),
    )(*raw)
    return xg, zg, cwg, cbg[0], xpg.T, dwg, dbg[0], alg.T, dsg[0], dgg[0]


def solution(mesh):
    placed = (
        P("seq", "chan"),
        P("seq", "chan"),
        P("seq", "chan"),
        P(None, "chan"),
        P("chan"),
        P("chan", None),
        P(None, "chan"),
        P("chan"),
        P("chan", None),
        P("chan"),
        P(),
    )
    counts = (mesh.shape["seq"], mesh.shape["chan"])
    return jax.shard_map(
        functools.partial(per_device, counts),
        mesh=mesh,
        in_specs=placed,
        out_specs=(
            P("seq", "chan"),
            P("seq", "chan"),
            P(None, "chan"),
            P("chan"),
            P("chan", None),
            P(None, "chan"),
            P("chan"),
            P("chan", None),
            P("chan"),
            P(),
        ),
        check_vma=False,
    )
```

```python
import functools
import math

import jax
import jax.numpy as jnp
from jax import lax
from jax.experimental import pallas as pl
from jax.experimental.pallas import tpu as pltpu
from jax.sharding import PartitionSpec as P

EPS = 1e-06
LOG2E = 1.4426950408889634
LANES = 128
GROUP = 16
F32 = jnp.float32
BF16 = jnp.bfloat16
MESH = pl.DeviceIdType.MESH
VMEM_BYTES = 60 * 1024 * 1024
CHUNK = 4


def dot(a, b):
    return jnp.dot(a, b, preferred_element_type=F32)


def dot_nt(a, b):
    return lax.dot_general(a, b, (((1,), (1,)), ((), ())), preferred_element_type=F32)


def dot_tn(a, b):
    return lax.dot_general(a, b, (((0,), (0,)), ((), ())), preferred_element_type=F32)


def iota(shape, dim):
    return lax.broadcasted_iota(jnp.int32, shape, dim)


def silu_grad(value):
    sigma = jax.nn.sigmoid(value)
    return sigma * (1.0 + value * (1.0 - sigma))


def softplus(value):
    return jnp.maximum(value, 0.0) + jnp.log1p(jnp.exp(-jnp.abs(value)))


class Exchange:
    def __init__(self, axis, count, me, send_sem, recv_sem):
        self.axis, self.count, self.me = axis, count, me
        self.send_sem, self.recv_sem = send_sem, recv_sem

    def _copy(self, src, dst, send, recv, peer):
        return pltpu.make_async_remote_copy(
            src_ref=src,
            dst_ref=dst,
            send_sem=self.send_sem.at[send],
            recv_sem=self.recv_sem.at[recv],
            device_id={self.axis: peer},
            device_id_type=MESH,
        )

    def peers(self):
        return [lax.rem(self.me + d, self.count) for d in range(1, self.count)]

    def send(self, src, dst, peer):
        self._copy(src, dst, peer, self.me, peer).start()

    def wait_recv(self, slot, peer):
        self._copy(slot, slot, peer, peer, peer).wait_recv()

    def wait_send(self, slot, peer):
        self._copy(slot, slot, peer, peer, peer).wait_send()


def layer_kernel(dims, *refs):
    T, C, NS, NC, R, N = dims
    hbm, refs = refs[:11], refs[11:]
    (xg_o, zg_o, dw_ag, xl_ag, sm_ag,
     x_ref, z_ref, g_ref, cw_ref, cb_ref, xw_ref, dw_ref, db_ref, al_ref, ds_ref, dg_ref,
     xpad, pre_act, act_slope, u_bf, gy, gz, part, send1, rs1, ag1, low_own, inv_own,
     pre_soft, delta, drive, bB, cB, a_buf, h0, h1, lam0, lam1, ha0, ha1,
     st_f, st_b, tot, in_f, in_b, in_tot, carry_f, carry_b,
     e_exp, m_b, m_c, sel_b, sel_c, dmask, back_b, back_c,
     b_diag, c_diag, b_all, c_all, adj_all, by_all, uscan, pregrad, prehalf, send2, rs2, ag2,
     dw_f, dw_send, dw_rs, xl_f, xl_send, xl_rs, sm_f, sm_own, sm_send, sm_rs,
     halo_x, halo_a, apad,
     s_in, s_c, r_c, s_st, r_st, s_sq, r_sq, s_h, r_h) = refs
    h_buf, lam_buf, ha_buf = (h0, h1), (lam0, lam1), (ha0, ha1)
    HC = C // 2
    HALVES = (slice(0, HC), slice(HC, C))
    ROWS = T // NC
    W = R + LANES
    P2 = R + 2 * N
    NB = T // GROUP
    GN = GROUP * N
    RB = R // NS
    SM = sm_f.shape[0]
    SB = 2 * SM // NS
    ms, mc = lax.axis_index("seq"), lax.axis_index("chan")

    def chan(k):
        return Exchange("chan", NC, mc, s_c.at[k], r_c.at[k])

    def seq(k):
        return Exchange("seq", NS, ms, s_sq.at[k], r_sq.at[k])

    def states(k):
        return Exchange("seq", NS, ms, s_st.at[k], r_st.at[k])

    barrier = pltpu.get_barrier_semaphore()
    for d in range(1, NC):
        pl.semaphore_signal(barrier, inc=1, device_id={"chan": lax.rem(mc + d, NC)}, device_id_type=MESH)
    for d in range(1, NS):
        pl.semaphore_signal(barrier, inc=1, device_id={"seq": lax.rem(ms + d, NS)}, device_id_type=MESH)
    local = (x_ref, z_ref, g_ref, cw_ref, cb_ref, xw_ref, dw_ref, db_ref, al_ref, ds_ref, dg_ref)
    fetch = [pltpu.make_async_copy(hbm[k], local[k], s_in.at[k]) for k in range(11)]
    for k in (0, 3, 4, 5, 1, 2, 6, 7, 8, 9, 10):
        fetch[k].start()

    xpad[:8, :] = jnp.zeros((8, C), F32)
    for k in (0, 3, 4):
        fetch[k].wait()
    xpad[8:, :] = x_ref[...].astype(F32)
    cw = cw_ref[...]

    def conv(first, count):
        total = jnp.broadcast_to(cb_ref[...], (count, C))
        for k in range(4):
            total = total + cw[k : k + 1] * xpad[first + 5 + k : first + 5 + k + count, :]
        pre_act[first : first + count, :] = total
        u_bf[first : first + count, :] = (total * jax.nn.sigmoid(total)).astype(BF16)

    def project(first, count):
        sums = dot_nt(u_bf[first : first + count, :], xw_ref[...])
        part[first : first + count, :R] = sums[:, :R]
        part[first : first + count, R:P2] = sums[:, R:P2]
        send1[first : first + count, :R] = sums[:, :R].astype(BF16)
        send1[first : first + count, R:P2] = sums[:, R:P2].astype(BF16)

    def halo_copy(src, dst, k, peer):
        return pltpu.make_async_remote_copy(
            src_ref=src, dst_ref=dst, send_sem=s_h.at[k], recv_sem=r_h.at[k],
            device_id={"seq": peer}, device_id_type=MESH,
        )

    def block(ref, i, size):
        return ref.at[pl.ds(pl.multiple_of(i * size, size), size), :]

    def scatter(ex, src, slots, size):
        for peer in ex.peers():
            ex.send(block(src, peer, size), slots.at[ex.me], peer)

    def collect(ex, slots, own):
        for peer in ex.peers():
            ex.wait_recv(slots.at[peer], peer)
        for peer in ex.peers():
            own = own + slots[peer].astype(F32)
        return own

    def spread(ex, buf, size):
        for peer in ex.peers():
            ex.send(block(buf, ex.me, size), block(buf, ex.me, size), peer)

    def arrive(ex, buf, size):
        for peer in ex.peers():
            ex.wait_recv(block(buf, peer, size), peer)

    after, before = lax.rem(ms + 1, NS), lax.rem(ms + NS - 1, NS)
    pl.semaphore_wait(barrier, NC + NS - 2)

    @pl.when(ms < NS - 1)
    def _():
        halo_copy(x_ref.at[T - 16 :, :], halo_x, 0, after).start()

    part[:, R:] = jnp.zeros((T, LANES), F32)
    send1[:, R:] = jnp.zeros((T, LANES), BF16)
    conv(0, T)
    fetch[5].wait()
    project(ROWS, T - ROWS)
    for peer in chan(0).peers():

        @pl.when(peer != 0)
        def _(peer=peer):
            chan(0).send(block(send1, peer, ROWS), rs1.at[mc], peer)

    @pl.when(ms > 0)
    def _():
        halo_copy(halo_x, halo_x, 0, before).wait_recv()
        xpad[:8, :] = halo_x[...].astype(F32)[8:16]
        conv(0, 16)

    project(0, ROWS)

    @pl.when(mc != 0)
    def _():
        chan(0).send(block(send1, 0, ROWS), rs1.at[mc], 0)

    for k in (1, 2, 6, 7, 8, 9, 10):
        fetch[k].wait()
    gate = z_ref[...].astype(F32)
    cot = g_ref[...].astype(F32)
    sig = jax.nn.sigmoid(gate)
    gy[...] = cot * gate * sig
    gz[...] = cot * sig * (1.0 + gate * (1.0 - sig))
    e_exp[...] = (iota((GN, GROUP), 0) // N == iota((GN, GROUP), 1)).astype(F32).astype(BF16)
    row_n, lane = iota((GN, LANES), 0) % N, iota((GN, LANES), 1)
    m_b[...] = ((lane == row_n) | (lane == row_n + 2 * N)).astype(F32)
    m_c[...] = ((lane == row_n + N) | (lane == row_n + 3 * N)).astype(F32)
    back_b[...] = (lane == row_n).astype(F32).astype(BF16)
    back_c[...] = (lane == row_n + N).astype(F32).astype(BF16)
    k_row, col_n = iota((LANES, GN), 0), iota((LANES, GN), 1) % N
    sel_b[...] = ((k_row == col_n) | (k_row == col_n + 2 * N)).astype(F32).astype(BF16)
    sel_c[...] = ((k_row == col_n + N) | (k_row == col_n + 3 * N)).astype(F32).astype(BF16)
    dmask[...] = (iota(dmask.shape, 1) // N == iota(dmask.shape, 0) % GROUP).astype(F32)
    rate = -jnp.exp(al_ref[...])
    rate2 = rate * LOG2E

    def my_rows(ref):
        return ref[pl.ds(pl.multiple_of(mc * ROWS, ROWS), ROWS), :]

    proj = collect(chan(0), rs1, my_rows(part))
    low = proj[:, :R]
    inv = lax.rsqrt(jnp.mean(low * low, -1, keepdims=True) + EPS)
    low_own[...] = low
    inv_own[...] = jnp.broadcast_to(inv, inv_own.shape)
    tail = proj[:, R:]
    tail_hi = tail.astype(BF16).astype(F32)
    tail = tail_hi + pltpu.roll(tail - tail_hi, 2 * N, 1)
    mine = pl.ds(pl.multiple_of(mc * ROWS, ROWS), ROWS)
    ag1[mine, :R] = (low * inv * dg_ref[...]).astype(BF16)
    ag1[mine, R:] = tail.astype(BF16)
    spread(chan(1), ag1, ROWS)
    arrive(chan(1), ag1, ROWS)

    def tokens(i, count=GROUP):
        return pl.ds(pl.multiple_of(i * count, count), count)

    soft = dot(ag1[:, :R], dw_ref[...]) + db_ref[...]
    pre_soft[...] = soft
    step = softplus(soft)
    delta[...] = step
    drive[...] = step * u_bf[...].astype(F32)
    tot[...] = jnp.sum(step, 0, keepdims=True)
    for peer in states(2).peers():
        states(2).send(tot, in_tot.at[ms], peer)

    ones = jnp.ones((LANES, LANES), BF16)

    def widen(out, mask):
        def some(i, carry):
            spread_rows = [dot(e_exp[...], ag1[tokens(i * CHUNK + k), R:]) for k in range(CHUNK)]
            for k in range(CHUNK):
                at = pl.ds(pl.multiple_of((i * CHUNK + k) * GN, GN), GN)
                out[at, :] = dot((spread_rows[k] * mask[...]).astype(BF16), ones)
            return carry

        lax.fori_loop(0, NB // CHUNK, some, 0)

    def rows_from(ref, first, count, sl=slice(None)):
        return ref.at[pl.ds(pl.multiple_of(first, 8), count), sl]

    def states_from(ref, first, count, sl=slice(None)):
        return ref.at[pl.ds(pl.multiple_of(first * N, 8 * N), count * N), sl]

    def row(view, j):
        return view[j : j + 1, :]

    def state(view, j):
        return view[j * N : (j + 1) * N, :]

    def wide(view, j, width):
        return jnp.concatenate([view[j * N : (j + 1) * N, :]] * (width // LANES), axis=1)

    zero_state = jnp.zeros((N, C), F32)
    rates = [rate[:, sl] for sl in HALVES]

    def forward_part(i, h):
        first = i * GROUP
        steps, drives = (rows_from(ref, first, GROUP) for ref in (delta, drive))
        decays, b_rows = (states_from(ref, first, GROUP) for ref in (a_buf, bB))
        for j in range(GROUP):
            a = jnp.exp2(row(steps, j) * rate2)
            decays[j * N : (j + 1) * N, :] = a
            h = a * h + row(drives, j) * wide(b_rows, j, C)
        return h

    def backward_part(i, g):
        first = T - GROUP * (i + 1)
        grads = rows_from(gy, first, GROUP)
        decays, c_rows = (states_from(ref, first, GROUP) for ref in (a_buf, cB))
        for j in reversed(range(GROUP)):
            g = state(decays, j) * (row(grads, j) * wide(c_rows, j, C) + g)
        return g

    def forward_carry():
        for peer in states(2).peers():
            states(2).wait_recv(in_tot.at[peer], peer)
        carry_f[...] = zero_state
        for s in range(NS - 1):

            @pl.when(s < ms)
            def _(s=s):
                states(0).wait_recv(in_f.at[s], s)
                carry_f[...] = jnp.exp2(in_tot[s] * rate2) * carry_f[...] + in_f[s].astype(F32)

    def backward_carry():
        carry_b[...] = zero_state
        for s in range(NS - 1, 0, -1):

            @pl.when(s > ms)
            def _(s=s):
                states(1).wait_recv(in_b.at[s], s)
                carry_b[...] = jnp.exp2(in_tot[s] * rate2) * carry_b[...] + in_b[s].astype(F32)

    def forward_block(hf, k, h):
        first = k * GROUP
        drives = rows_from(drive, first, GROUP, HALVES[hf])
        decays, b_rows = states_from(a_buf, first, GROUP, HALVES[hf]), states_from(bB, first, GROUP)
        later = h_buf[hf].at[pl.ds(pl.multiple_of(first * N + N, N), GROUP * N), :]
        for j in range(GROUP):
            h = state(decays, j) * h + row(drives, j) * wide(b_rows, j, HC)
            later[j * N : (j + 1) * N, :] = h.astype(BF16)
        return h

    def start_states(hf):
        start = carry_f[:, HALVES[hf]]
        h_buf[hf][:N, :] = start.astype(BF16)
        return start

    def state_rows(hf, k):
        return h_buf[hf][pl.ds(pl.multiple_of(k * GN + N, N), GN), :]

    def adjoint_rows(buf, k):
        return buf[pl.ds(pl.multiple_of(k * GN, GN), GN), :]

    def backward_block(hf, k, g):
        sl = HALVES[hf]
        first = k * GROUP
        grads = rows_from(gy, first, GROUP, sl)
        befores, lams, has = (states_from(ref[hf], first, GROUP) for ref in (h_buf, lam_buf, ha_buf))
        decays = states_from(a_buf, first, GROUP, sl)
        c_rows = states_from(cB, first, GROUP)
        for j in reversed(range(GROUP)):
            lam = row(grads, j) * wide(c_rows, j, HC) + g
            g = state(decays, j) * lam
            hold = g * state(befores, j).astype(F32)
            lams[j * N : (j + 1) * N, :] = lam.astype(BF16)
            has[j * N : (j + 1) * N, :] = (hold * rates[hf]).astype(BF16)
        return g

    def state_sums(hf, k):
        lam_rows = adjoint_rows(lam_buf[hf], k)
        adj_b = dot(b_diag[tokens(k), :], lam_rows)
        by_rate = dot(dmask[:GROUP, :].astype(BF16), adjoint_rows(ha_buf[hf], k))
        return adj_b, by_rate, dot_nt(drive[tokens(k), HALVES[hf]].astype(BF16), lam_rows)

    def c_sums(hf, k):
        return dot_nt(gy[tokens(k), HALVES[hf]].astype(BF16), state_rows(hf, k))

    def half_grads(hf, at, adj_b, by_rate):
        sl = HALVES[hf]
        pre = (by_rate + adj_b * u_bf[at, sl].astype(F32)) * jax.nn.sigmoid(pre_soft[at, sl])
        pregrad[at, sl] = pre
        prehalf[at, sl] = pre.astype(BF16)
        uscan[at, sl] = ds_ref[:, sl] * gy[at, sl] + delta[at, sl] * adj_b

    widen(bB, m_b)
    st_f[...] = lax.fori_loop(0, NB, forward_part, zero_state).astype(BF16)
    for d in range(1, NS):

        @pl.when(ms + d < NS)
        def _(d=d):
            states(0).send(st_f, in_f.at[ms], ms + d)

    widen(cB, m_c)
    st_b[...] = lax.fori_loop(0, NB, backward_part, zero_state).astype(BF16)
    for d in range(1, NS):

        @pl.when(ms - d >= 0)
        def _(d=d):
            states(1).send(st_b, in_b.at[ms], ms - d)

    act_slope[...] = silu_grad(pre_act[...])
    mask = (iota((T, GN), 1) // N == iota((T, GN), 0) % GROUP).astype(F32)
    b_diag[...] = (dot(ag1[:, R:], sel_b[...]) * mask).astype(BF16)
    c_diag[...] = (dot(ag1[:, R:], sel_c[...]) * mask).astype(BF16)

    def states_both(i, carry):
        g, h = carry
        c_all[tokens(i), :] = c_sums(0, i)
        return backward_block(0, NB - 1 - i, g), forward_block(1, i, h)

    forward_carry()
    lax.fori_loop(0, NB, functools.partial(forward_block, 0), start_states(0))
    backward_carry()
    lax.fori_loop(0, NB, states_both, (carry_b[:, HALVES[0]], start_states(1)))
    CT = CHUNK * GROUP

    def backward_chunk(i, g):
        c = NB // CHUNK - 1 - i

        def backward_second(m, g):
            k = c * CHUNK + CHUNK - 1 - m
            at = tokens(k)
            adj_all[at, :], by_all[at, :], b_all[at, :] = state_sums(0, k)
            c_all[at, :] = c_all[at, :] + c_sums(1, k)
            return backward_block(1, k, g)

        g = lax.fori_loop(0, CHUNK, backward_second, g)
        at = tokens(c, CT)
        sums = [state_sums(1, c * CHUNK + k) for k in range(CHUNK)]
        half_grads(0, at, adj_all[at, :], by_all[at, :])
        b_cols = (c_all[at, :] * dmask[...]).astype(BF16)
        tail = dot(b_cols, back_c[...])
        adj_b, by_rate, b_sums = (jnp.concatenate(parts, 0) for parts in zip(*sums))
        half_grads(1, at, adj_b, by_rate)
        b_cols = ((b_all[at, :] + b_sums) * dmask[...]).astype(BF16)
        tail = tail + dot(b_cols, back_b[...])
        normed = dot_nt(prehalf[at, :], dw_ref[...])
        part[at, :R] = normed
        part[at, R:] = tail
        send2[at, :R] = normed.astype(BF16)
        send2[at, R:] = tail.astype(BF16)
        for k in range(CHUNK):
            owner = c * CHUNK + k

            @pl.when(owner != mc)
            def _(owner=owner):
                chan(2).send(block(send2, owner, ROWS), rs2.at[mc], owner)

        return g

    lax.fori_loop(0, NB // CHUNK, backward_chunk, carry_b[:, HALVES[1]])

    dw_f[...] = dot_tn(ag1[:, :R], prehalf[...])
    dw_send[...] = dw_f[...].astype(BF16)
    scatter(seq(0), dw_send, dw_rs, RB)

    def outputs(i, carry):
        y = []
        for k in range(CHUNK):
            k = i * CHUNK + k
            y.append(jnp.concatenate([dot(c_diag[tokens(k), :], state_rows(hf, k)) for hf in range(2)], 1))
        at = tokens(i, CT)
        y = jnp.concatenate(y, 0) + ds_ref[...] * u_bf[at, :].astype(F32)
        zg_o[at, :] = (gz[at, :] * y).astype(BF16)
        return carry

    lax.fori_loop(0, NB // CHUNK, outputs, 0)

    for hf in range(2):

        def rate_part(i, acc):
            steps = rows_from(delta, i * GROUP, GROUP, HALVES[hf])
            has = states_from(ha_buf[hf], i * GROUP, GROUP)
            for j in range(GROUP):
                acc = acc + row(steps, j) * state(has, j).astype(F32)
            return acc

        sm_f[2 * N : 3 * N, HALVES[hf]] = lax.fori_loop(0, NB, rate_part, zero_state[:, :HC])
    sm_f[3 * N :, :] = jnp.zeros((SM - 3 * N, C), F32)
    sm_f[3 * N + 5 : 3 * N + 6, :] = jnp.sum(pregrad[...], 0, keepdims=True)
    sm_f[3 * N + 6 : 3 * N + 7, :] = jnp.sum(gy[...] * u_bf[...].astype(F32), 0, keepdims=True)

    grad_rows = collect(chan(2), rs2, my_rows(part))
    low = low_own[...]
    inv = inv_own[:, :1]
    scaled = grad_rows[:, :R] * dg_ref[...]
    low_grad = inv * scaled - low * (inv * inv * inv) * jnp.mean(scaled * low, -1, keepdims=True)
    gain = jnp.sum(grad_rows[:, :R] * low * inv, 0, keepdims=True)
    half = LANES // 2
    lanes = iota((ROWS, LANES), 1)
    rows = iota((ROWS, LANES), 0)
    g0 = jnp.broadcast_to(gain[:, :LANES], (ROWS, LANES))
    g1 = jnp.broadcast_to(gain[:, LANES:], (ROWS, LANES))
    q = rows % 4
    gq = jnp.where(q == 0, pltpu.roll(g0, half, 1), jnp.where(q == 1, g0, jnp.where(q == 2, pltpu.roll(g1, half, 1), g1)))
    g_hi = gq.astype(BF16).astype(F32)
    g_rows = jnp.where(rows < 4, g_hi, jnp.where(rows < 8, gq - g_hi, 0.0))
    ag2[mine, :R] = low_grad.astype(BF16)
    ag2[mine, R:] = jnp.where(lanes < half, grad_rows[:, R:], g_rows).astype(BF16)
    spread(chan(3), ag2, ROWS)

    own = collect(seq(0), dw_rs, dw_f[pl.ds(pl.multiple_of(ms * RB, RB), RB), :])
    dw_ag[pl.ds(pl.multiple_of(ms * RB, RB), RB), :] = own.astype(BF16)
    spread(seq(1), dw_ag, RB)

    arrive(chan(3), ag2, ROWS)

    xl_f[...] = dot_tn(ag2[...], u_bf[...])
    xl_send[...] = xl_f[:R, :].astype(BF16)
    scatter(seq(2), xl_send, xl_rs, RB)
    sm_f[: 2 * N, :] = xl_f[R:P2, :]
    total = uscan[...] + dot(ag2[:, :R], xw_ref[:R, :]) + dot(ag2[:, R:P2], xw_ref[R:, :])
    act_grad = total * act_slope[...]
    apad[:T, :] = act_grad
    apad[T:, :] = jnp.zeros((8, C), F32)

    @pl.when(ms > 0)
    def _():
        halo_copy(apad.at[:8, :], halo_a, 1, before).start()

    for k in range(4):
        sm_f[3 * N + k : 3 * N + k + 1, :] = jnp.sum(act_grad * xpad[5 + k : 5 + k + T, :], 0, keepdims=True)
    sm_f[3 * N + 4 : 3 * N + 5, :] = jnp.sum(act_grad, 0, keepdims=True)
    g_sum = jnp.zeros((ROWS, LANES), F32)
    for c in range(NC):
        g_sum = g_sum + ag2[c * ROWS : (c + 1) * ROWS, R:].astype(F32)
    gq = g_sum[:4] + g_sum[4:8]
    low_half = iota((1, LANES), 1) < half
    for k in range(2):
        sm_f[3 * N + 7 : 3 * N + 8, k * LANES : (k + 1) * LANES] = jnp.where(
            low_half, pltpu.roll(gq[2 * k : 2 * k + 1], half, 1), gq[2 * k + 1 : 2 * k + 2]
        )
    for k in range(2):
        sm_own[k * SM : (k + 1) * SM, :] = sm_f[:, k * HC : (k + 1) * HC]
    sm_send[...] = sm_own[...].astype(BF16)
    scatter(seq(3), sm_send, sm_rs, SB)

    @pl.when(ms < NS - 1)
    def _():
        halo_copy(halo_a, halo_a, 1, after).wait_recv()
        apad[T:, :] = halo_a[...]

    total = jnp.zeros((T, C), F32)
    for k in range(4):
        total = total + cw[k : k + 1] * apad[3 - k : 3 - k + T, :]
    xg_o[...] = total.astype(BF16)

    at = pl.ds(pl.multiple_of(ms * RB, RB), RB)
    xl_ag[at, :] = collect(seq(2), xl_rs, xl_f[at, :]).astype(BF16)
    spread(seq(4), xl_ag, RB)
    at = pl.ds(pl.multiple_of(ms * SB, SB), SB)
    sm_ag[at, :] = collect(seq(3), sm_rs, sm_own[at, :]).astype(BF16)
    spread(seq(5), sm_ag, SB)
    arrive(seq(1), dw_ag, RB)
    arrive(seq(4), xl_ag, RB)
    arrive(seq(5), sm_ag, SB)

    for k, size, src in ((0, ROWS, send1), (1, ROWS, ag1), (2, ROWS, send2), (3, ROWS, ag2)):
        for peer in chan(k).peers():
            chan(k).wait_send(src.at[:size, :], peer)
    for k, size, src in ((0, RB, dw_send), (1, RB, dw_ag), (2, RB, xl_send), (3, SB, sm_send), (4, RB, xl_ag), (5, SB, sm_ag)):
        for peer in seq(k).peers():
            seq(k).wait_send(src.at[:size, :], peer)
    for peer in states(2).peers():
        states(2).wait_send(tot, peer)
    for d in range(1, NS):

        @pl.when(ms + d < NS)
        def _(d=d):
            states(0).wait_send(st_f, ms + d)

        @pl.when(ms - d >= 0)
        def _(d=d):
            states(1).wait_send(st_b, ms - d)

    @pl.when(ms < NS - 1)
    def _():
        halo_copy(halo_x, halo_x, 0, after).wait_send()

    @pl.when(ms > 0)
    def _():
        halo_copy(halo_a, halo_a, 1, before).wait_send()


def finish_kernel(dims, xg, zg, dw_sum, xl_sum, sm_sum, xg_o, zg_o, cwg_o, cbg_o, xpg_o, dwg_o, dbg_o, alg_o, dsg_o, dgg_o):
    T, C, NS, NC, R, N = dims
    scale = 1.0 / math.sqrt(T * NS)
    xg_o[...] = xg[...]
    zg_o[...] = zg[...]
    dwg_o[...] = scale * dw_sum[...].astype(F32)
    xpg_o[:R, :] = scale * xl_sum[...].astype(F32)
    HC = C // 2
    small = scale * sm_sum[...].astype(F32)
    for hf in range(2):
        sl = slice(hf * HC, (hf + 1) * HC)
        rows = small[hf * 4 * N : (hf + 1) * 4 * N]
        xpg_o[R:, sl] = rows[: 2 * N]
        alg_o[:, sl] = rows[2 * N : 3 * N]
        cwg_o[:, sl] = rows[3 * N : 3 * N + 4]
        cbg_o[:, sl] = rows[3 * N + 4 : 3 * N + 5]
        dbg_o[:, sl] = rows[3 * N + 5 : 3 * N + 6]
        dsg_o[:, sl] = rows[3 * N + 6 : 3 * N + 7]
        if hf * HC < R:
            dgg_o[:, sl] = rows[3 * N + 7 : 3 * N + 8]


def per_device(counts, x_in, z_in, grad_out, conv_w, conv_b, xproj_w, dt_w, dt_bias, a_log, d_skip, dt_gain):
    T, C = x_in.shape
    R = dt_w.shape[0]
    N = a_log.shape[1]
    NS, NC = counts
    ROWS = T // NC
    W = R + LANES
    GN = GROUP * N
    SM = 4 * N
    HC = C // 2
    dims = (T, C, NS, NC, R, N)

    def f32(*shape):
        return pltpu.VMEM(shape, F32)

    def b16(*shape):
        return pltpu.VMEM(shape, BF16)

    dma = pltpu.SemaphoreType.DMA
    scratch = dict(
        x_ref=b16(T, C), z_ref=b16(T, C), g_ref=b16(T, C), cw_ref=f32(4, C), cb_ref=f32(1, C), xw_ref=b16(R + 2 * N, C),
        dw_ref=b16(R, C), db_ref=f32(1, C), al_ref=f32(N, C), ds_ref=f32(1, C), dg_ref=f32(1, R),
        xpad=f32(T + 8, C), pre_act=f32(T, C), act_slope=f32(T, C), u_bf=b16(T, C), gy=f32(T, C), gz=f32(T, C),
        part=f32(T, W), send1=b16(T, W), rs1=b16(NC, ROWS, W), ag1=b16(T, W),
        low_own=f32(ROWS, R), inv_own=f32(ROWS, LANES),
        pre_soft=f32(T, C), delta=f32(T, C), drive=f32(T, C), bB=f32(T * N, LANES), cB=f32(T * N, LANES),
        a_buf=f32(T * N, C), h0=b16((T + 1) * N, HC), h1=b16((T + 1) * N, HC),
        lam0=b16(T * N, HC), lam1=b16(T * N, HC), ha0=b16(T * N, HC), ha1=b16(T * N, HC),
        st_f=b16(N, C), st_b=b16(N, C), tot=f32(1, C), in_f=b16(NS, N, C), in_b=b16(NS, N, C),
        in_tot=f32(NS, 1, C), carry_f=f32(N, C), carry_b=f32(N, C),
        e_exp=b16(GN, GROUP), m_b=f32(GN, LANES), m_c=f32(GN, LANES), sel_b=b16(LANES, GN), sel_c=b16(LANES, GN),
        dmask=f32(CHUNK * GROUP, GN), back_b=b16(GN, LANES), back_c=b16(GN, LANES),
        b_diag=b16(T, GN), c_diag=b16(T, GN), b_all=f32(T, GN), c_all=f32(T, GN), adj_all=f32(T, HC), by_all=f32(T, HC),
        uscan=f32(T, C), pregrad=f32(T, C), prehalf=b16(T, C),
        send2=b16(T, W), rs2=b16(NC, ROWS, W), ag2=b16(T, W),
        dw_f=f32(R, C), dw_send=b16(R, C), dw_rs=b16(NS, R // NS, C),
        xl_f=f32(W, C), xl_send=b16(R, C), xl_rs=b16(NS, R // NS, C),
        sm_f=f32(SM, C), sm_own=f32(2 * SM, HC), sm_send=b16(2 * SM, HC), sm_rs=b16(NS, 2 * SM // NS, HC),
        halo_x=b16(16, C), halo_a=f32(8, C), apad=f32(T + 8, C),
        s_in=dma((11,)), s_c=dma((4, NC)), r_c=dma((4, NC)), s_st=dma((3, NS)), r_st=dma((3, NS)),
        s_sq=dma((6, NS)), r_sq=dma((6, NS)), s_h=dma((2,)), r_h=dma((2,)),
    )
    S = jax.ShapeDtypeStruct
    vmem = pl.BlockSpec(memory_space=pltpu.VMEM)
    raw = pl.pallas_call(
        functools.partial(layer_kernel, dims),
        out_shape=(S((T, C), BF16), S((T, C), BF16), S((R, C), BF16), S((R, C), BF16), S((2 * SM, HC), BF16)),
        in_specs=[pl.BlockSpec(memory_space=pl.ANY)] * 11,
        out_specs=(vmem,) * 5,
        scratch_shapes=list(scratch.values()),
        compiler_params=pltpu.CompilerParams(
            collective_id=0, has_side_effects=True, vmem_limit_bytes=VMEM_BYTES
        ),
    )(
        x_in, z_in, grad_out, conv_w, conv_b[None], xproj_w.T, dt_w, dt_bias[None], a_log.T, d_skip[None], dt_gain[None],
    )
    xg, zg, cwg, cbg, xpg, dwg, dbg, alg, dsg, dgg = pl.pallas_call(
        functools.partial(finish_kernel, dims),
        out_shape=(
            S((T, C), BF16), S((T, C), BF16), S((4, C), F32), S((1, C), F32), S((R + 2 * N, C), F32),
            S((R, C), F32), S((1, C), F32), S((N, C), F32), S((1, C), F32), S((1, R), F32),
        ),
        in_specs=[vmem] * 5,
        out_specs=(vmem,) * 10,
        compiler_params=pltpu.CompilerParams(vmem_limit_bytes=VMEM_BYTES),
    )(*raw)
    return xg, zg, cwg, cbg[0], xpg.T, dwg, dbg[0], alg.T, dsg[0], dgg[0]


def solution(mesh):
    placed = (
        P("seq", "chan"),
        P("seq", "chan"),
        P("seq", "chan"),
        P(None, "chan"),
        P("chan"),
        P("chan", None),
        P(None, "chan"),
        P("chan"),
        P("chan", None),
        P("chan"),
        P(),
    )
    counts = (mesh.shape["seq"], mesh.shape["chan"])
    return jax.shard_map(
        functools.partial(per_device, counts),
        mesh=mesh,
        in_specs=placed,
        out_specs=(
            P("seq", "chan"),
            P("seq", "chan"),
            P(None, "chan"),
            P("chan"),
            P("chan", None),
            P(None, "chan"),
            P("chan"),
            P("chan", None),
            P("chan"),
            P(),
        ),
        check_vma=False,
    )
```

```python
import functools
import math

import jax
import jax.numpy as jnp
from jax import lax
from jax.experimental import pallas as pl
from jax.experimental.pallas import tpu as pltpu
from jax.sharding import PartitionSpec as P

EPS = 1e-06
LOG2E = 1.4426950408889634
LANES = 128
GROUP = 16
F32 = jnp.float32
BF16 = jnp.bfloat16
MESH = pl.DeviceIdType.MESH
VMEM_BYTES = 60 * 1024 * 1024
CHUNK = 4


def dot(a, b):
    return jnp.dot(a, b, preferred_element_type=F32)


def dot_nt(a, b):
    return lax.dot_general(a, b, (((1,), (1,)), ((), ())), preferred_element_type=F32)


def dot_tn(a, b):
    return lax.dot_general(a, b, (((0,), (0,)), ((), ())), preferred_element_type=F32)


def iota(shape, dim):
    return lax.broadcasted_iota(jnp.int32, shape, dim)


def silu_grad(value):
    sigma = jax.nn.sigmoid(value)
    return sigma * (1.0 + value * (1.0 - sigma))


def softplus(value):
    return jnp.maximum(value, 0.0) + jnp.log1p(jnp.exp(-jnp.abs(value)))


class Exchange:
    def __init__(self, axis, count, me, send_sem, recv_sem):
        self.axis, self.count, self.me = axis, count, me
        self.send_sem, self.recv_sem = send_sem, recv_sem

    def _copy(self, src, dst, send, recv, peer):
        return pltpu.make_async_remote_copy(
            src_ref=src,
            dst_ref=dst,
            send_sem=self.send_sem.at[send],
            recv_sem=self.recv_sem.at[recv],
            device_id={self.axis: peer},
            device_id_type=MESH,
        )

    def peers(self):
        minor = 4 if self.axis == "chan" else 2
        major = self.count // minor
        steps = [(a, b) for a in range(major) for b in range(minor) if (a, b) != (0, 0)]
        steps.sort(key=lambda s: -min(s[0], major - s[0]) - min(s[1], minor - s[1]))
        return [
            lax.rem(self.me // minor + a, major) * minor + lax.rem(lax.rem(self.me, minor) + b, minor)
            for a, b in steps
        ]

    def send(self, src, dst, peer):
        self._copy(src, dst, peer, self.me, peer).start()

    def wait_recv(self, slot, peer):
        self._copy(slot, slot, peer, peer, peer).wait_recv()

    def wait_send(self, slot, peer):
        self._copy(slot, slot, peer, peer, peer).wait_send()


def layer_kernel(dims, *refs):
    T, C, NS, NC, R, N = dims
    hbm, refs = refs[:11], refs[11:]
    (xg_o, zg_o, dw_o, xl_ag, sm_ag,
     x_ref, z_ref, g_ref, cw_ref, cb_ref, xw_ref, dw_ref, db_ref, al_ref, ds_ref, dg_ref,
     xg_v, zg_v, dw_ag, shifts, shifted, first_parts, pre_act, act_slope, u_bf, gy, gz, part, send1, rs1, ag1, low_own, inv_own,
     pre_soft, delta, drive, bB, cB, a_buf, h0, h1, lam0, lam1, ha0, ha1,
     st_f, st_b, tot, in_f, in_b, in_tot, carry_f, carry_b,
     e_exp, m_b, m_c, sel_b, sel_c, dmask, back_b, back_c,
     tail32, b_diag, c_diag, b_all, c_all, adj_all, by_all, uscan, pregrad, prehalf, send2, rs2, ag2,
     dw_f, dw_send, dw_rs, xl_f, xl_send, xl_rs, sm_f, sm_own, sm_send, sm_rs,
     halo_x, halo_a, apad,
     s_in, s_out, s_c, r_c, s_st, r_st, s_sq, r_sq, s_h, r_h) = refs
    h_buf, lam_buf, ha_buf = (h0, h1), (lam0, lam1), (ha0, ha1)
    HC = C // 2
    HALVES = (slice(0, HC), slice(HC, C))
    ROWS = T // NC
    W = R + LANES
    P2 = R + 2 * N
    NB = T // GROUP
    GN = GROUP * N
    RB = R // NS
    SM = sm_f.shape[0]
    SB = 2 * SM // NS
    ms, mc = lax.axis_index("seq"), lax.axis_index("chan")

    def chan(k):
        return Exchange("chan", NC, mc, s_c.at[k], r_c.at[k])

    def seq(k):
        return Exchange("seq", NS, ms, s_sq.at[k], r_sq.at[k])

    def states(k):
        return Exchange("seq", NS, ms, s_st.at[k], r_st.at[k])

    barrier = pltpu.get_barrier_semaphore()
    for peer in chan(0).peers():
        pl.semaphore_signal(barrier, inc=1, device_id={"chan": peer}, device_id_type=MESH)
    for peer in seq(0).peers():
        pl.semaphore_signal(barrier, inc=1, device_id={"seq": peer}, device_id_type=MESH)
    local = (x_ref, z_ref, g_ref, cw_ref, cb_ref, xw_ref, dw_ref, db_ref, al_ref, ds_ref, dg_ref)
    fetch = [pltpu.make_async_copy(hbm[k], local[k], s_in.at[k]) for k in range(11)]
    for k in (0, 3, 4, 5, 1, 2, 6, 7, 8, 9, 10):
        fetch[k].start()

    for k in range(3):
        shifts[k * T : (k + 1) * T, :] = (iota((T, T), 1) == iota((T, T), 0) + (k - 3)).astype(F32).astype(BF16)
    part[:, R:] = jnp.zeros((T, LANES), F32)
    send1[:, R:] = jnp.zeros((T, LANES), BF16)
    for k in (0, 3, 4):
        fetch[k].wait()
    cw = cw_ref[...]
    shifted[...] = dot(shifts[...], x_ref[...]).astype(BF16)

    def conv(first, count):
        for r in range(first, first + count, 16):
            total = cb_ref[...] + cw[3:4] * x_ref[r : r + 16, :].astype(F32)
            for k in range(3):
                total = total + cw[k : k + 1] * shifted[k * T + r : k * T + r + 16, :].astype(F32)
            pre_act[r : r + 16, :] = total
            u_bf[r : r + 16, :] = (total * jax.nn.sigmoid(total)).astype(BF16)

    def project(first, count):
        sums = dot_nt(u_bf[first : first + count, :], xw_ref[...])
        part[first : first + count, :R] = sums[:, :R]
        part[first : first + count, R:P2] = sums[:, R:P2]
        send1[first : first + count, :R] = sums[:, :R].astype(BF16)
        send1[first : first + count, R:P2] = sums[:, R:P2].astype(BF16)

    conv(ROWS, T - ROWS)
    fetch[5].wait()
    project(ROWS, T - ROWS)

    def halo_copy(src, dst, k, peer):
        return pltpu.make_async_remote_copy(
            src_ref=src, dst_ref=dst, send_sem=s_h.at[k], recv_sem=r_h.at[k],
            device_id={"seq": peer}, device_id_type=MESH,
        )

    def block(ref, i, size):
        return ref.at[pl.ds(pl.multiple_of(i * size, size), size), :]

    def scatter(ex, src, slots, size):
        for peer in ex.peers():
            ex.send(block(src, peer, size), slots.at[ex.me], peer)

    def collect(ex, slots, own):
        for peer in ex.peers():
            ex.wait_recv(slots.at[peer], peer)
        for peer in ex.peers():
            own = own + slots[peer].astype(F32)
        return own

    def spread(ex, buf, size):
        for peer in ex.peers():
            ex.send(block(buf, ex.me, size), block(buf, ex.me, size), peer)

    def arrive(ex, buf, size):
        for peer in ex.peers():
            ex.wait_recv(block(buf, peer, size), peer)

    after, before = lax.rem(ms + 1, NS), lax.rem(ms + NS - 1, NS)
    pl.semaphore_wait(barrier, NC + NS - 2)

    @pl.when(ms < NS - 1)
    def _():
        halo_copy(x_ref.at[T - 16 :, :], halo_x, 0, after).start()

    for peer in chan(0).peers():

        @pl.when(peer != 0)
        def _(peer=peer):
            chan(0).send(block(send1, peer, ROWS), rs1.at[mc], peer)

    for k in (1, 2, 6, 7, 8, 9, 10):
        fetch[k].wait()
    gate = z_ref[...].astype(F32)
    cot = g_ref[...].astype(F32)
    sig = jax.nn.sigmoid(gate)
    gy[...] = cot * gate * sig
    gz[...] = cot * sig * (1.0 + gate * (1.0 - sig))
    e_exp[...] = (iota((GN, GROUP), 0) // N == iota((GN, GROUP), 1)).astype(F32).astype(BF16)
    row_n, lane = iota((GN, LANES), 0) % N, iota((GN, LANES), 1)
    m_b[...] = ((lane == row_n) | (lane == row_n + 2 * N)).astype(F32)
    m_c[...] = ((lane == row_n + N) | (lane == row_n + 3 * N)).astype(F32)
    back_b[...] = (lane == row_n).astype(F32).astype(BF16)
    back_c[...] = (lane == row_n + N).astype(F32).astype(BF16)
    k_row, col_n = iota((LANES, GN), 0), iota((LANES, GN), 1) % N
    sel_b[...] = ((k_row == col_n) | (k_row == col_n + 2 * N)).astype(F32).astype(BF16)
    sel_c[...] = ((k_row == col_n + N) | (k_row == col_n + 3 * N)).astype(F32).astype(BF16)
    dmask[...] = (iota(dmask.shape, 1) // N == iota(dmask.shape, 0) % GROUP).astype(F32)
    rate = -jnp.exp(al_ref[...])
    rate2 = rate * LOG2E

    @pl.when(ms == 0)
    def _():
        halo_x[...] = jnp.zeros_like(halo_x)

    @pl.when(ms > 0)
    def _():
        halo_copy(halo_x, halo_x, 0, before).wait_recv()

    window = jnp.concatenate([halo_x[...], x_ref[:16, :]], 0)
    near = iota((48, 32), 0)
    near = (iota((48, 32), 1) == near % 16 + near // 16 + 13).astype(F32).astype(BF16)
    near = dot(near, window).astype(BF16)
    for k in range(3):
        shifted[k * T : k * T + 16, :] = near[16 * k : 16 * k + 16]
    conv(0, ROWS)
    project(0, ROWS)
    first_parts[mc] = send1[:ROWS, :]
    for peer in chan(4).peers():
        chan(4).send(first_parts.at[mc], first_parts.at[mc], peer)

    mine = pl.ds(pl.multiple_of(mc * ROWS, ROWS), ROWS)

    def my_rows(ref):
        return ref[mine, :]

    def normed_rows(proj):
        low = proj[:, :R]
        inv = lax.rsqrt(jnp.mean(low * low, -1, keepdims=True) + EPS)
        tail = proj[:, R:]
        tail_hi = tail.astype(BF16).astype(F32)
        tail = tail_hi + pltpu.roll(tail - tail_hi, 2 * N, 1)
        return low, inv, (low * inv * dg_ref[...]).astype(BF16), tail.astype(BF16)

    def keep(low, inv):
        low_own[...] = low
        inv_own[...] = jnp.broadcast_to(inv, inv_own.shape)

    @pl.when(mc != 0)
    def _():
        low, inv, ag1[mine, :R], ag1[mine, R:] = normed_rows(collect(chan(0), rs1, my_rows(part)))
        spread(chan(1), ag1, ROWS)
        keep(low, inv)

    for peer in chan(4).peers():
        chan(4).wait_recv(first_parts.at[peer], peer)
    proj = jnp.zeros((ROWS, W), F32)
    for c in range(NC):
        proj = proj + first_parts[c].astype(F32)
    low, inv, ag1[:ROWS, :R], ag1[:ROWS, R:] = normed_rows(proj)

    @pl.when(mc == 0)
    def _():
        keep(low, inv)

    for peer in chan(1).peers():

        @pl.when(peer != 0)
        def _(peer=peer):
            chan(1).wait_recv(block(ag1, peer, ROWS), peer)

    def tokens(i, count=GROUP):
        return pl.ds(pl.multiple_of(i * count, count), count)

    pre_soft[...] = dot(ag1[:, :R], dw_ref[...])
    steps_sum = jnp.zeros((16, C), F32)
    for r in range(0, T, 16):
        soft = pre_soft[r : r + 16, :] + db_ref[...]
        pre_soft[r : r + 16, :] = soft
        step = softplus(soft)
        delta[r : r + 16, :] = step
        drive[r : r + 16, :] = step * u_bf[r : r + 16, :].astype(F32)
        steps_sum = steps_sum + step
    tot[...] = jnp.sum(steps_sum, 0, keepdims=True)
    for peer in states(2).peers():
        states(2).send(tot, in_tot.at[ms], peer)

    ones = jnp.ones((LANES, LANES), BF16)

    tail32[...] = ag1[:, R:].astype(F32)

    def widen(out, mask):
        def some(i, carry):
            rows = tail32.at[tokens(i, CHUNK * GROUP), :]
            spread_rows = [(rows[j : j + 1, :] * mask[:N, :]).astype(BF16) for j in range(CHUNK * GROUP)]
            out[pl.ds(pl.multiple_of(i * CHUNK * GN, GN), CHUNK * GN), :] = dot(jnp.concatenate(spread_rows, 0), ones)
            return carry

        lax.fori_loop(0, NB // CHUNK, some, 0)

    def rows_from(ref, first, count, sl=slice(None)):
        return ref.at[pl.ds(pl.multiple_of(first, 8), count), sl]

    def states_from(ref, first, count, sl=slice(None)):
        return ref.at[pl.ds(pl.multiple_of(first * N, 8 * N), count * N), sl]

    def row(view, j):
        return view[j : j + 1, :]

    def state(view, j):
        return view[j * N : (j + 1) * N, :]

    def wide(view, j, width):
        return jnp.concatenate([view[j * N : (j + 1) * N, :]] * (width // LANES), axis=1)

    zero_state = jnp.zeros((N, C), F32)
    rates = [rate[:, sl] for sl in HALVES]

    def forward_part(i, h):
        first = i * GROUP
        steps, drives = (rows_from(ref, first, GROUP) for ref in (delta, drive))
        decays, b_rows = (states_from(ref, first, GROUP) for ref in (a_buf, bB))
        for j in range(GROUP):
            a = jnp.exp2(row(steps, j) * rate2)
            decays[j * N : (j + 1) * N, :] = a
            h = a * h + row(drives, j) * wide(b_rows, j, C)
        return h

    def backward_part(i, g):
        first = T - GROUP * (i + 1)
        grads = rows_from(gy, first, GROUP)
        decays, c_rows = (states_from(ref, first, GROUP) for ref in (a_buf, cB))
        for j in reversed(range(GROUP)):
            g = state(decays, j) * (row(grads, j) * wide(c_rows, j, C) + g)
        return g

    def forward_carry():
        for peer in states(2).peers():
            states(2).wait_recv(in_tot.at[peer], peer)
        carry_f[...] = zero_state
        for s in range(NS - 1):

            @pl.when(s < ms)
            def _(s=s):
                states(0).wait_recv(in_f.at[s], s)
                carry_f[...] = jnp.exp2(in_tot[s] * rate2) * carry_f[...] + in_f[s].astype(F32)

    def backward_carry():
        carry_b[...] = zero_state
        for s in range(NS - 1, 0, -1):

            @pl.when(s > ms)
            def _(s=s):
                states(1).wait_recv(in_b.at[s], s)
                carry_b[...] = jnp.exp2(in_tot[s] * rate2) * carry_b[...] + in_b[s].astype(F32)

    def forward_block(hf, k, h):
        first = k * GROUP
        drives = rows_from(drive, first, GROUP, HALVES[hf])
        decays, b_rows = states_from(a_buf, first, GROUP, HALVES[hf]), states_from(bB, first, GROUP)
        later = h_buf[hf].at[pl.ds(pl.multiple_of(first * N + N, N), GROUP * N), :]
        for j in range(GROUP):
            h = state(decays, j) * h + row(drives, j) * wide(b_rows, j, HC)
            later[j * N : (j + 1) * N, :] = h.astype(BF16)
        return h

    def start_states(hf):
        start = carry_f[:, HALVES[hf]]
        h_buf[hf][:N, :] = start.astype(BF16)
        return start

    def state_rows(hf, k):
        return h_buf[hf][pl.ds(pl.multiple_of(k * GN + N, N), GN), :]

    def adjoint_rows(buf, k):
        return buf[pl.ds(pl.multiple_of(k * GN, GN), GN), :]

    def backward_block(hf, k, g):
        sl = HALVES[hf]
        first = k * GROUP
        grads = rows_from(gy, first, GROUP, sl)
        befores, lams, has = (states_from(ref[hf], first, GROUP) for ref in (h_buf, lam_buf, ha_buf))
        decays = states_from(a_buf, first, GROUP, sl)
        c_rows = states_from(cB, first, GROUP)
        for j in reversed(range(GROUP)):
            lam = row(grads, j) * wide(c_rows, j, HC) + g
            g = state(decays, j) * lam
            hold = g * state(befores, j).astype(F32)
            lams[j * N : (j + 1) * N, :] = lam.astype(BF16)
            has[j * N : (j + 1) * N, :] = (hold * rates[hf]).astype(BF16)
        return g

    def state_sums(hf, k):
        lam_rows = adjoint_rows(lam_buf[hf], k)
        adj_b = dot(b_diag[tokens(k), :], lam_rows)
        by_rate = dot(dmask[:GROUP, :].astype(BF16), adjoint_rows(ha_buf[hf], k))
        return adj_b, by_rate, dot_nt(drive[tokens(k), HALVES[hf]].astype(BF16), lam_rows)

    def c_sums(hf, k):
        return dot_nt(gy[tokens(k), HALVES[hf]].astype(BF16), state_rows(hf, k))

    def half_grads(hf, at, adj_b, by_rate):
        sl = HALVES[hf]
        pre = (by_rate + adj_b * u_bf[at, sl].astype(F32)) * jax.nn.sigmoid(pre_soft[at, sl])
        pregrad[at, sl] = pre
        prehalf[at, sl] = pre.astype(BF16)
        uscan[at, sl] = ds_ref[:, sl] * gy[at, sl] + delta[at, sl] * adj_b

    widen(bB, m_b)
    st_f[...] = lax.fori_loop(0, NB, forward_part, zero_state).astype(BF16)
    for d in range(NS - 1, 0, -1):

        @pl.when(ms + d < NS)
        def _(d=d):
            states(0).send(st_f, in_f.at[ms], ms + d)

    widen(cB, m_c)
    st_b[...] = lax.fori_loop(0, NB, backward_part, zero_state).astype(BF16)
    for d in range(NS - 1, 0, -1):

        @pl.when(ms - d >= 0)
        def _(d=d):
            states(1).send(st_b, in_b.at[ms], ms - d)

    act_slope[...] = silu_grad(pre_act[...])
    mask = (iota((T, GN), 1) // N == iota((T, GN), 0) % GROUP).astype(F32)
    b_diag[...] = (dot(ag1[:, R:], sel_b[...]) * mask).astype(BF16)
    c_diag[...] = (dot(ag1[:, R:], sel_c[...]) * mask).astype(BF16)

    def states_both(i, carry):
        g, h = carry
        for k in range(2):
            k = 2 * i + k
            c_all[tokens(k), :] = c_sums(0, k)
            g, h = backward_block(0, NB - 1 - k, g), forward_block(1, k, h)
        return g, h

    forward_carry()
    lax.fori_loop(0, NB, functools.partial(forward_block, 0), start_states(0))
    backward_carry()
    lax.fori_loop(0, NB // 2, states_both, (carry_b[:, HALVES[0]], start_states(1)))
    CT = CHUNK * GROUP

    def backward_chunk(i, g):
        c = NB // CHUNK - 1 - i

        def backward_second(m, g):
            k = c * CHUNK + CHUNK - 1 - m
            at = tokens(k)
            adj_all[at, :], by_all[at, :], b_all[at, :] = state_sums(0, k)
            c_all[at, :] = c_all[at, :] + c_sums(1, k)
            return backward_block(1, k, g)

        for m in range(CHUNK):
            g = backward_second(m, g)
        at = tokens(c, CT)
        sums = [state_sums(1, c * CHUNK + k) for k in range(CHUNK)]
        half_grads(0, at, adj_all[at, :], by_all[at, :])
        b_cols = (c_all[at, :] * dmask[...]).astype(BF16)
        tail = dot(b_cols, back_c[...])
        adj_b, by_rate, b_sums = (jnp.concatenate(parts, 0) for parts in zip(*sums))
        half_grads(1, at, adj_b, by_rate)
        b_cols = ((b_all[at, :] + b_sums) * dmask[...]).astype(BF16)
        tail = tail + dot(b_cols, back_b[...])
        normed = dot_nt(prehalf[at, :], dw_ref[...])
        part[at, :R] = normed
        part[at, R:] = tail
        send2[at, :R] = normed.astype(BF16)
        send2[at, R:] = tail.astype(BF16)
        for k in range(CHUNK):
            owner = c * CHUNK + k

            @pl.when(owner != mc)
            def _(owner=owner):
                chan(2).send(block(send2, owner, ROWS), rs2.at[mc], owner)

        return g

    lax.fori_loop(0, NB // CHUNK, backward_chunk, carry_b[:, HALVES[1]])

    dw_f[...] = dot_tn(ag1[:, :R], prehalf[...])
    dw_send[...] = dw_f[...].astype(BF16)
    scatter(seq(0), dw_send, dw_rs, RB)

    def outputs(i, carry):
        y = []
        for k in range(CHUNK):
            k = i * CHUNK + k
            y.append(jnp.concatenate([dot(c_diag[tokens(k), :], state_rows(hf, k)) for hf in range(2)], 1))
        at = tokens(i, CT)
        y = jnp.concatenate(y, 0) + ds_ref[...] * u_bf[at, :].astype(F32)
        zg_v[at, :] = (gz[at, :] * y).astype(BF16)
        return carry

    lax.fori_loop(0, NB // CHUNK, outputs, 0)
    leave = [pltpu.make_async_copy(v, o, s_out.at[k]) for k, (v, o) in enumerate(((zg_v, zg_o), (xg_v, xg_o), (dw_ag, dw_o)))]
    leave[0].start()

    for hf in range(2):

        def rate_part(i, acc):
            steps = rows_from(delta, i * GROUP, GROUP, HALVES[hf])
            has = states_from(ha_buf[hf], i * GROUP, GROUP)
            for j in range(GROUP):
                acc = acc + row(steps, j) * state(has, j).astype(F32)
            return acc

        sm_f[2 * N : 3 * N, HALVES[hf]] = lax.fori_loop(0, NB, rate_part, zero_state[:, :HC])
    sm_f[3 * N :, :] = jnp.zeros((SM - 3 * N, C), F32)
    sm_f[3 * N + 5 : 3 * N + 6, :] = jnp.sum(pregrad[...], 0, keepdims=True)
    sm_f[3 * N + 6 : 3 * N + 7, :] = jnp.sum(gy[...] * u_bf[...].astype(F32), 0, keepdims=True)

    grad_rows = collect(chan(2), rs2, my_rows(part))
    low = low_own[...]
    inv = inv_own[:, :1]
    scaled = grad_rows[:, :R] * dg_ref[...]
    low_grad = inv * scaled - low * (inv * inv * inv) * jnp.mean(scaled * low, -1, keepdims=True)
    gain = jnp.sum(grad_rows[:, :R] * low * inv, 0, keepdims=True)
    half = LANES // 2
    lanes = iota((ROWS, LANES), 1)
    rows = iota((ROWS, LANES), 0)
    g0 = jnp.broadcast_to(gain[:, :LANES], (ROWS, LANES))
    g1 = jnp.broadcast_to(gain[:, LANES:], (ROWS, LANES))
    q = rows % 4
    gq = jnp.where(q == 0, pltpu.roll(g0, half, 1), jnp.where(q == 1, g0, jnp.where(q == 2, pltpu.roll(g1, half, 1), g1)))
    g_hi = gq.astype(BF16).astype(F32)
    g_rows = jnp.where(rows < 4, g_hi, jnp.where(rows < 8, gq - g_hi, 0.0))
    ag2[mine, :R] = low_grad.astype(BF16)
    ag2[mine, R:] = jnp.where(lanes < half, grad_rows[:, R:], g_rows).astype(BF16)
    spread(chan(3), ag2, ROWS)

    own = collect(seq(0), dw_rs, dw_f[pl.ds(pl.multiple_of(ms * RB, RB), RB), :])
    dw_ag[pl.ds(pl.multiple_of(ms * RB, RB), RB), :] = own.astype(BF16)
    spread(seq(1), dw_ag, RB)

    arrive(chan(3), ag2, ROWS)

    PB = RB // 2

    def piece(ref, i, p):
        return ref.at[pl.ds(pl.multiple_of(i * RB + p * PB, PB), PB), :]

    xl_f[...] = dot_tn(ag2[...], u_bf[...])
    xl_send[...] = xl_f[:R, :].astype(BF16)
    for p in range(2):
        for peer in seq(2 + p).peers():
            seq(2 + p).send(piece(xl_send, peer, p), xl_rs.at[p, ms], peer)
    sm_f[: 2 * N, :] = xl_f[R:P2, :]
    total = uscan[...] + dot(ag2[:, :R], xw_ref[:R, :]) + dot(ag2[:, R:P2], xw_ref[R:, :])
    apad[:T, :] = total * act_slope[...]
    apad[T:, :] = jnp.zeros((8, C), F32)

    @pl.when(ms > 0)
    def _():
        halo_copy(apad.at[:8, :], halo_a, 1, before).start()

    sums = [jnp.zeros((16, C), F32) for _ in range(5)]
    for r in range(0, T, 16):
        grad = apad[r : r + 16, :]
        for k in range(3):
            sums[k] = sums[k] + grad * shifted[k * T + r : k * T + r + 16, :].astype(F32)
        sums[3] = sums[3] + grad * x_ref[r : r + 16, :].astype(F32)
        sums[4] = sums[4] + grad
    for k in range(5):
        sm_f[3 * N + k : 3 * N + k + 1, :] = jnp.sum(sums[k], 0, keepdims=True)
    g_sum = jnp.zeros((ROWS, LANES), F32)
    for c in range(NC):
        g_sum = g_sum + ag2[c * ROWS : (c + 1) * ROWS, R:].astype(F32)
    gq = g_sum[:4] + g_sum[4:8]
    low_half = iota((1, LANES), 1) < half
    for k in range(2):
        sm_f[3 * N + 7 : 3 * N + 8, k * LANES : (k + 1) * LANES] = jnp.where(
            low_half, pltpu.roll(gq[2 * k : 2 * k + 1], half, 1), gq[2 * k + 1 : 2 * k + 2]
        )
    for k in range(2):
        sm_own[k * SM : (k + 1) * SM, :] = sm_f[:, k * HC : (k + 1) * HC]
    sm_send[...] = sm_own[...].astype(BF16)
    scatter(seq(4), sm_send, sm_rs, SB)

    @pl.when(ms < NS - 1)
    def _():
        halo_copy(halo_a, halo_a, 1, after).wait_recv()
        apad[T:, :] = halo_a[...]

    for r in range(0, T, 32):
        total = cw[3:4] * apad[r : r + 32, :]
        for k in range(3):
            total = total + cw[k : k + 1] * apad[r + 3 - k : r + 3 - k + 32, :]
        xg_v[r : r + 32, :] = total.astype(BF16)
    leave[1].start()
    arrive(seq(1), dw_ag, RB)
    leave[2].start()

    for k, size, src in ((0, ROWS, send1), (1, ROWS, ag1), (2, ROWS, send2), (3, ROWS, ag2), (4, ROWS, send1)):
        for peer in chan(k).peers():
            if k == 0:
                pl.when(peer != 0)(functools.partial(chan(k).wait_send, src.at[:size, :], peer))
            elif k == 1:
                pl.when(mc != 0)(functools.partial(chan(k).wait_send, src.at[:size, :], peer))
            else:
                chan(k).wait_send(src.at[:size, :], peer)
    for k, src in ((0, dw_send), (1, dw_ag)):
        for peer in seq(k).peers():
            seq(k).wait_send(src.at[:RB, :], peer)
    for peer in states(2).peers():
        states(2).wait_send(tot, peer)
    for d in range(1, NS):

        @pl.when(ms + d < NS)
        def _(d=d):
            states(0).wait_send(st_f, ms + d)

        @pl.when(ms - d >= 0)
        def _(d=d):
            states(1).wait_send(st_b, ms - d)

    @pl.when(ms < NS - 1)
    def _():
        halo_copy(halo_x, halo_x, 0, after).wait_send()

    @pl.when(ms > 0)
    def _():
        halo_copy(halo_a, halo_a, 1, before).wait_send()

    for p in range(2):
        at = pl.ds(pl.multiple_of(ms * RB + p * PB, PB), PB)
        xl_ag[at, :] = collect(seq(2 + p), xl_rs.at[p], xl_f[at, :]).astype(BF16)
        for peer in seq(5 + p).peers():
            seq(5 + p).send(piece(xl_ag, ms, p), piece(xl_ag, ms, p), peer)
    at = pl.ds(pl.multiple_of(ms * SB, SB), SB)
    sm_ag[at, :] = collect(seq(4), sm_rs, sm_own[at, :]).astype(BF16)
    spread(seq(7), sm_ag, SB)
    for copy in leave:
        copy.wait()
    for k, size, src in ((2, PB, xl_send), (3, PB, xl_send), (4, SB, sm_send)):
        for peer in seq(k).peers():
            seq(k).wait_send(src.at[:size, :], peer)
    for p in range(2):
        for peer in seq(5 + p).peers():
            seq(5 + p).wait_recv(piece(xl_ag, peer, p), peer)
    arrive(seq(7), sm_ag, SB)
    for k, size, src in ((5, PB, xl_ag), (6, PB, xl_ag), (7, SB, sm_ag)):
        for peer in seq(k).peers():
            seq(k).wait_send(src.at[:size, :], peer)


def finish_kernel(dims, xg, zg, dw_sum, xl_sum, sm_sum, xg_o, zg_o, cwg_o, cbg_o, xpg_o, dwg_o, dbg_o, alg_o, dsg_o, dgg_o):
    T, C, NS, NC, R, N = dims
    scale = 1.0 / math.sqrt(T * NS)
    xg_o[...] = xg[...]
    zg_o[...] = zg[...]
    dwg_o[...] = scale * dw_sum[...].astype(F32)
    xpg_o[:R, :] = scale * xl_sum[...].astype(F32)
    HC = C // 2
    small = scale * sm_sum[...].astype(F32)
    for hf in range(2):
        sl = slice(hf * HC, (hf + 1) * HC)
        rows = small[hf * 4 * N : (hf + 1) * 4 * N]
        xpg_o[R:, sl] = rows[: 2 * N]
        alg_o[:, sl] = rows[2 * N : 3 * N]
        cwg_o[:, sl] = rows[3 * N : 3 * N + 4]
        cbg_o[:, sl] = rows[3 * N + 4 : 3 * N + 5]
        dbg_o[:, sl] = rows[3 * N + 5 : 3 * N + 6]
        dsg_o[:, sl] = rows[3 * N + 6 : 3 * N + 7]
        if hf * HC < R:
            dgg_o[:, sl] = rows[3 * N + 7 : 3 * N + 8]


def per_device(counts, x_in, z_in, grad_out, conv_w, conv_b, xproj_w, dt_w, dt_bias, a_log, d_skip, dt_gain):
    T, C = x_in.shape
    R = dt_w.shape[0]
    N = a_log.shape[1]
    NS, NC = counts
    ROWS = T // NC
    W = R + LANES
    GN = GROUP * N
    SM = 4 * N
    HC = C // 2
    dims = (T, C, NS, NC, R, N)

    def f32(*shape):
        return pltpu.VMEM(shape, F32)

    def b16(*shape):
        return pltpu.VMEM(shape, BF16)

    dma = pltpu.SemaphoreType.DMA
    scratch = dict(
        x_ref=b16(T, C), z_ref=b16(T, C), g_ref=b16(T, C), cw_ref=f32(4, C), cb_ref=f32(1, C), xw_ref=b16(R + 2 * N, C),
        dw_ref=b16(R, C), db_ref=f32(1, C), al_ref=f32(N, C), ds_ref=f32(1, C), dg_ref=f32(1, R),
        xg_v=b16(T, C), zg_v=b16(T, C), dw_ag=b16(R, C), shifts=b16(3 * T, T), shifted=b16(3 * T, C),
        first_parts=b16(NC, ROWS, W), pre_act=f32(T, C), act_slope=f32(T, C), u_bf=b16(T, C), gy=f32(T, C), gz=f32(T, C),
        part=f32(T, W), send1=b16(T, W), rs1=b16(NC, ROWS, W), ag1=b16(T, W),
        low_own=f32(ROWS, R), inv_own=f32(ROWS, LANES),
        pre_soft=f32(T, C), delta=f32(T, C), drive=f32(T, C), bB=f32(T * N, LANES), cB=f32(T * N, LANES),
        a_buf=f32(T * N, C), h0=b16((T + 1) * N, HC), h1=b16((T + 1) * N, HC),
        lam0=b16(T * N, HC), lam1=b16(T * N, HC), ha0=b16(T * N, HC), ha1=b16(T * N, HC),
        st_f=b16(N, C), st_b=b16(N, C), tot=f32(1, C), in_f=b16(NS, N, C), in_b=b16(NS, N, C),
        in_tot=f32(NS, 1, C), carry_f=f32(N, C), carry_b=f32(N, C),
        e_exp=b16(GN, GROUP), m_b=f32(GN, LANES), m_c=f32(GN, LANES), sel_b=b16(LANES, GN), sel_c=b16(LANES, GN),
        dmask=f32(CHUNK * GROUP, GN), back_b=b16(GN, LANES), back_c=b16(GN, LANES),
        tail32=f32(T, LANES), b_diag=b16(T, GN), c_diag=b16(T, GN), b_all=f32(T, GN), c_all=f32(T, GN), adj_all=f32(T, HC), by_all=f32(T, HC),
        uscan=f32(T, C), pregrad=f32(T, C), prehalf=b16(T, C),
        send2=b16(T, W), rs2=b16(NC, ROWS, W), ag2=b16(T, W),
        dw_f=f32(R, C), dw_send=b16(R, C), dw_rs=b16(NS, R // NS, C),
        xl_f=f32(W, C), xl_send=b16(R, C), xl_rs=b16(2, NS, R // NS // 2, C),
        sm_f=f32(SM, C), sm_own=f32(2 * SM, HC), sm_send=b16(2 * SM, HC), sm_rs=b16(NS, 2 * SM // NS, HC),
        halo_x=b16(16, C), halo_a=f32(8, C), apad=f32(T + 8, C),
        s_in=dma((11,)), s_out=dma((3,)), s_c=dma((5, NC)), r_c=dma((5, NC)), s_st=dma((3, NS)), r_st=dma((3, NS)),
        s_sq=dma((8, NS)), r_sq=dma((8, NS)), s_h=dma((2,)), r_h=dma((2,)),
    )
    S = jax.ShapeDtypeStruct
    vmem = pl.BlockSpec(memory_space=pltpu.VMEM)
    raw = pl.pallas_call(
        functools.partial(layer_kernel, dims),
        out_shape=(S((T, C), BF16), S((T, C), BF16), S((R, C), BF16), S((R, C), BF16), S((2 * SM, HC), BF16)),
        in_specs=[pl.BlockSpec(memory_space=pl.ANY)] * 11,
        out_specs=(pl.BlockSpec(memory_space=pl.ANY),) * 3 + (vmem,) * 2,
        scratch_shapes=list(scratch.values()),
        compiler_params=pltpu.CompilerParams(
            collective_id=0, has_side_effects=True, vmem_limit_bytes=VMEM_BYTES
        ),
    )(
        x_in, z_in, grad_out, conv_w, conv_b[None], xproj_w.T, dt_w, dt_bias[None], a_log.T, d_skip[None], dt_gain[None],
    )
    xg, zg, cwg, cbg, xpg, dwg, dbg, alg, dsg, dgg = pl.pallas_call(
        functools.partial(finish_kernel, dims),
        out_shape=(
            S((T, C), BF16), S((T, C), BF16), S((4, C), F32), S((1, C), F32), S((R + 2 * N, C), F32),
            S((R, C), F32), S((1, C), F32), S((N, C), F32), S((1, C), F32), S((1, R), F32),
        ),
        in_specs=[vmem] * 5,
        out_specs=(vmem,) * 10,
        compiler_params=pltpu.CompilerParams(vmem_limit_bytes=VMEM_BYTES),
    )(*raw)
    return xg, zg, cwg, cbg[0], xpg.T, dwg, dbg[0], alg.T, dsg[0], dgg[0]


def solution(mesh):
    placed = (
        P("seq", "chan"),
        P("seq", "chan"),
        P("seq", "chan"),
        P(None, "chan"),
        P("chan"),
        P("chan", None),
        P(None, "chan"),
        P("chan"),
        P("chan", None),
        P("chan"),
        P(),
    )
    counts = (mesh.shape["seq"], mesh.shape["chan"])
    return jax.shard_map(
        functools.partial(per_device, counts),
        mesh=mesh,
        in_specs=placed,
        out_specs=(
            P("seq", "chan"),
            P("seq", "chan"),
            P(None, "chan"),
            P("chan"),
            P("chan", None),
            P(None, "chan"),
            P("chan"),
            P("chan", None),
            P("chan"),
            P(),
        ),
        check_vma=False,
    )
```

```python
import functools
import math

import jax
import jax.numpy as jnp
from jax import lax
from jax.experimental import pallas as pl
from jax.experimental.pallas import tpu as pltpu
from jax.sharding import PartitionSpec as P

EPS = 1e-06
LOG2E = 1.4426950408889634
LANES = 128
GROUP = 16
F32 = jnp.float32
BF16 = jnp.bfloat16
MESH = pl.DeviceIdType.MESH
VMEM_BYTES = 60 * 1024 * 1024
CHUNK = 16


def dot(a, b):
    return jnp.dot(a, b, preferred_element_type=F32)


def dot_nt(a, b):
    return lax.dot_general(a, b, (((1,), (1,)), ((), ())), preferred_element_type=F32)


def dot_tn(a, b):
    return lax.dot_general(a, b, (((0,), (0,)), ((), ())), preferred_element_type=F32)


def iota(shape, dim):
    return lax.broadcasted_iota(jnp.int32, shape, dim)


def silu_grad(value):
    sigma = jax.nn.sigmoid(value)
    return sigma * (1.0 + value * (1.0 - sigma))


def softplus(value):
    return jnp.maximum(value, 0.0) + jnp.log1p(jnp.exp(-jnp.abs(value)))


class Exchange:
    def __init__(self, axis, count, me, send_sem, recv_sem):
        self.axis, self.count, self.me = axis, count, me
        self.send_sem, self.recv_sem = send_sem, recv_sem

    def _copy(self, src, dst, send, recv, peer):
        return pltpu.make_async_remote_copy(
            src_ref=src,
            dst_ref=dst,
            send_sem=self.send_sem.at[send],
            recv_sem=self.recv_sem.at[recv],
            device_id={self.axis: peer},
            device_id_type=MESH,
        )

    def peers(self):
        minor = 4 if self.axis == "chan" else 2
        major = self.count // minor
        steps = [(a, b) for a in range(major) for b in range(minor) if (a, b) != (0, 0)]
        steps.sort(key=lambda s: -min(s[0], major - s[0]) - min(s[1], minor - s[1]))
        return [
            lax.rem(self.me // minor + a, major) * minor + lax.rem(lax.rem(self.me, minor) + b, minor)
            for a, b in steps
        ]

    def send(self, src, dst, peer):
        self._copy(src, dst, peer, self.me, peer).start()

    def wait_recv(self, slot, peer):
        self._copy(slot, slot, peer, peer, peer).wait_recv()

    def wait_send(self, slot, peer):
        self._copy(slot, slot, peer, peer, peer).wait_send()


def layer_kernel(dims, *refs):
    T, C, NS, NC, R, N = dims
    hbm, refs = refs[:11], refs[11:]
    (xg_o, zg_o, dw_o, xl_ag, sm_ag,
     x_ref, z_ref, g_ref, cw_ref, cb_ref, xw_ref, dw_ref, db_ref, al_ref, ds_ref, dg_ref,
     xg_v, zg_v, dw_ag, shifts, shifted, first_parts, pre_act, act_slope, u_bf, gy, gz, part, send1, rs1, ag1, low_own, inv_own,
     pre_soft, delta, drive, bB, cB, a_buf, h0, h1, lam0, lam1, ha0, ha1,
     st_f, st_b, tot, in_f, in_b, in_tot, carry_f, carry_b,
     e_exp, m_b, m_c, sel_b, sel_c, dmask, back_b, back_c,
     tail32, b_diag, c_diag, b_all, c_all, adj_all, by_all, uscan, pregrad, prehalf, send2, rs2, ag2,
     dw_f, dw_send, dw_rs, xl_f, xl_send, xl_rs, sm_f, sm_own, sm_send, sm_rs,
     halo_x, halo_a, apad,
     s_in, s_out, s_c, r_c, s_st, r_st, s_sq, r_sq, s_h, r_h) = refs
    h_buf, lam_buf, ha_buf = (h0, h1), (lam0, lam1), (ha0, ha1)
    HC = C // 2
    HALVES = (slice(0, HC), slice(HC, C))
    ROWS = T // NC
    W = R + LANES
    P2 = R + 2 * N
    NB = T // GROUP
    GN = GROUP * N
    RB = R // NS
    SM = sm_f.shape[0]
    SB = 2 * SM // NS
    ms, mc = lax.axis_index("seq"), lax.axis_index("chan")

    def chan(k):
        return Exchange("chan", NC, mc, s_c.at[k], r_c.at[k])

    def seq(k):
        return Exchange("seq", NS, ms, s_sq.at[k], r_sq.at[k])

    def states(k):
        return Exchange("seq", NS, ms, s_st.at[k], r_st.at[k])

    barrier = pltpu.get_barrier_semaphore()
    for peer in chan(0).peers():
        pl.semaphore_signal(barrier, inc=1, device_id={"chan": peer}, device_id_type=MESH)
    for peer in seq(0).peers():
        pl.semaphore_signal(barrier, inc=1, device_id={"seq": peer}, device_id_type=MESH)
    local = (x_ref, z_ref, g_ref, cw_ref, cb_ref, xw_ref, dw_ref, db_ref, al_ref, ds_ref, dg_ref)
    fetch = [pltpu.make_async_copy(hbm[k], local[k], s_in.at[k]) for k in range(11)]
    for k in (0, 3, 4, 5, 1, 2, 6, 7, 8, 9, 10):
        fetch[k].start()

    for k in range(3):
        shifts[k * T : (k + 1) * T, :] = (iota((T, T), 1) == iota((T, T), 0) + (k - 3)).astype(F32).astype(BF16)
    part[:, R:] = jnp.zeros((T, LANES), F32)
    send1[:, R:] = jnp.zeros((T, LANES), BF16)
    for k in (0, 3, 4):
        fetch[k].wait()
    cw = cw_ref[...]
    shifted[...] = dot(shifts[...], x_ref[...]).astype(BF16)

    def conv(first, count):
        for r in range(first, first + count, 16):
            total = cb_ref[...] + cw[3:4] * x_ref[r : r + 16, :].astype(F32)
            for k in range(3):
                total = total + cw[k : k + 1] * shifted[k * T + r : k * T + r + 16, :].astype(F32)
            pre_act[r : r + 16, :] = total
            u_bf[r : r + 16, :] = (total * jax.nn.sigmoid(total)).astype(BF16)

    def project(first, count):
        sums = dot_nt(u_bf[first : first + count, :], xw_ref[...])
        part[first : first + count, :R] = sums[:, :R]
        part[first : first + count, R:P2] = sums[:, R:P2]
        send1[first : first + count, :R] = sums[:, :R].astype(BF16)
        send1[first : first + count, R:P2] = sums[:, R:P2].astype(BF16)

    conv(ROWS, T - ROWS)
    fetch[5].wait()
    project(ROWS, T - ROWS)

    def halo_copy(src, dst, k, peer):
        return pltpu.make_async_remote_copy(
            src_ref=src, dst_ref=dst, send_sem=s_h.at[k], recv_sem=r_h.at[k],
            device_id={"seq": peer}, device_id_type=MESH,
        )

    def block(ref, i, size):
        return ref.at[pl.ds(pl.multiple_of(i * size, size), size), :]

    def scatter(ex, src, slots, size):
        for peer in ex.peers():
            ex.send(block(src, peer, size), slots.at[ex.me], peer)

    def collect(ex, slots, own):
        for peer in ex.peers():
            ex.wait_recv(slots.at[peer], peer)
        for peer in ex.peers():
            own = own + slots[peer].astype(F32)
        return own

    def spread(ex, buf, size):
        for peer in ex.peers():
            ex.send(block(buf, ex.me, size), block(buf, ex.me, size), peer)

    def arrive(ex, buf, size):
        for peer in ex.peers():
            ex.wait_recv(block(buf, peer, size), peer)

    after, before = lax.rem(ms + 1, NS), lax.rem(ms + NS - 1, NS)
    pl.semaphore_wait(barrier, NC + NS - 2)

    @pl.when(ms < NS - 1)
    def _():
        halo_copy(x_ref.at[T - 16 :, :], halo_x, 0, after).start()

    for peer in chan(0).peers():

        @pl.when(peer != 0)
        def _(peer=peer):
            chan(0).send(block(send1, peer, ROWS), rs1.at[mc], peer)

    for k in (1, 2, 6, 7, 8, 9, 10):
        fetch[k].wait()
    gate = z_ref[...].astype(F32)
    cot = g_ref[...].astype(F32)
    sig = jax.nn.sigmoid(gate)
    gy[...] = cot * gate * sig
    gz[...] = cot * sig * (1.0 + gate * (1.0 - sig))
    e_exp[...] = (iota((GN, GROUP), 0) // N == iota((GN, GROUP), 1)).astype(F32).astype(BF16)
    row_n, lane = iota((GN, LANES), 0) % N, iota((GN, LANES), 1)
    m_b[...] = ((lane == row_n) | (lane == row_n + 2 * N)).astype(F32)
    m_c[...] = ((lane == row_n + N) | (lane == row_n + 3 * N)).astype(F32)
    back_b[...] = (lane == row_n).astype(F32).astype(BF16)
    back_c[...] = (lane == row_n + N).astype(F32).astype(BF16)
    k_row, col_n = iota((LANES, GN), 0), iota((LANES, GN), 1) % N
    sel_b[...] = ((k_row == col_n) | (k_row == col_n + 2 * N)).astype(F32).astype(BF16)
    sel_c[...] = ((k_row == col_n + N) | (k_row == col_n + 3 * N)).astype(F32).astype(BF16)
    dmask[...] = (iota(dmask.shape, 1) // N == iota(dmask.shape, 0) % GROUP).astype(F32)
    rate = -jnp.exp(al_ref[...])
    rate2 = rate * LOG2E

    @pl.when(ms == 0)
    def _():
        halo_x[...] = jnp.zeros_like(halo_x)

    @pl.when(ms > 0)
    def _():
        halo_copy(halo_x, halo_x, 0, before).wait_recv()

    window = jnp.concatenate([halo_x[...], x_ref[:16, :]], 0)
    near = iota((48, 32), 0)
    near = (iota((48, 32), 1) == near % 16 + near // 16 + 13).astype(F32).astype(BF16)
    near = dot(near, window).astype(BF16)
    for k in range(3):
        shifted[k * T : k * T + 16, :] = near[16 * k : 16 * k + 16]
    conv(0, ROWS)
    project(0, ROWS)
    first_parts[mc] = send1[:ROWS, :]
    for peer in chan(4).peers():
        chan(4).send(first_parts.at[mc], first_parts.at[mc], peer)

    mine = pl.ds(pl.multiple_of(mc * ROWS, ROWS), ROWS)

    def my_rows(ref):
        return ref[mine, :]

    def normed_rows(proj):
        low = proj[:, :R]
        inv = lax.rsqrt(jnp.mean(low * low, -1, keepdims=True) + EPS)
        tail = proj[:, R:]
        tail_hi = tail.astype(BF16).astype(F32)
        tail = tail_hi + pltpu.roll(tail - tail_hi, 2 * N, 1)
        return low, inv, (low * inv * dg_ref[...]).astype(BF16), tail.astype(BF16)

    def keep(low, inv):
        low_own[...] = low
        inv_own[...] = jnp.broadcast_to(inv, inv_own.shape)

    @pl.when(mc != 0)
    def _():
        low, inv, ag1[mine, :R], ag1[mine, R:] = normed_rows(collect(chan(0), rs1, my_rows(part)))
        spread(chan(1), ag1, ROWS)
        keep(low, inv)

    for peer in chan(4).peers():
        chan(4).wait_recv(first_parts.at[peer], peer)
    proj = jnp.zeros((ROWS, W), F32)
    for c in range(NC):
        proj = proj + first_parts[c].astype(F32)
    low, inv, ag1[:ROWS, :R], ag1[:ROWS, R:] = normed_rows(proj)

    @pl.when(mc == 0)
    def _():
        keep(low, inv)

    for peer in chan(1).peers():

        @pl.when(peer != 0)
        def _(peer=peer):
            chan(1).wait_recv(block(ag1, peer, ROWS), peer)

    def tokens(i, count=GROUP):
        return pl.ds(pl.multiple_of(i * count, count), count)

    pre_soft[...] = dot(ag1[:, :R], dw_ref[...])
    steps_sum = jnp.zeros((16, C), F32)
    for r in range(0, T, 16):
        soft = pre_soft[r : r + 16, :] + db_ref[...]
        pre_soft[r : r + 16, :] = soft
        step = softplus(soft)
        delta[r : r + 16, :] = step
        drive[r : r + 16, :] = step * u_bf[r : r + 16, :].astype(F32)
        steps_sum = steps_sum + step
    tot[...] = jnp.sum(steps_sum, 0, keepdims=True)
    for peer in states(2).peers():
        states(2).send(tot, in_tot.at[ms], peer)

    ones = jnp.ones((LANES, LANES), BF16)

    tail32[...] = ag1[:, R:].astype(F32)

    def widen(out, mask):
        def some(i, carry):
            rows = tail32.at[tokens(i, CHUNK * GROUP), :]
            spread_rows = [(rows[j : j + 1, :] * mask[:N, :]).astype(BF16) for j in range(CHUNK * GROUP)]
            out[pl.ds(pl.multiple_of(i * CHUNK * GN, GN), CHUNK * GN), :] = dot(jnp.concatenate(spread_rows, 0), ones)
            return carry

        lax.fori_loop(0, NB // CHUNK, some, 0)

    def rows_from(ref, first, count, sl=slice(None)):
        return ref.at[pl.ds(pl.multiple_of(first, 8), count), sl]

    def states_from(ref, first, count, sl=slice(None)):
        return ref.at[pl.ds(pl.multiple_of(first * N, 8 * N), count * N), sl]

    def row(view, j):
        return view[j : j + 1, :]

    def state(view, j):
        return view[j * N : (j + 1) * N, :]

    def wide(view, j, width):
        return jnp.concatenate([view[j * N : (j + 1) * N, :]] * (width // LANES), axis=1)

    zero_state = jnp.zeros((N, C), F32)
    rates = [rate[:, sl] for sl in HALVES]

    def forward_part(i, h):
        first = i * GROUP
        steps, drives = (rows_from(ref, first, GROUP) for ref in (delta, drive))
        decays, b_rows = (states_from(ref, first, GROUP) for ref in (a_buf, bB))
        for j in range(GROUP):
            a = jnp.exp2(row(steps, j) * rate2)
            decays[j * N : (j + 1) * N, :] = a
            h = a * h + row(drives, j) * wide(b_rows, j, C)
        return h

    def backward_part(i, g):
        first = T - GROUP * (i + 1)
        grads = rows_from(gy, first, GROUP)
        decays, c_rows = (states_from(ref, first, GROUP) for ref in (a_buf, cB))
        for j in reversed(range(GROUP)):
            g = state(decays, j) * (row(grads, j) * wide(c_rows, j, C) + g)
        return g

    def forward_carry():
        for peer in states(2).peers():
            states(2).wait_recv(in_tot.at[peer], peer)
        carry_f[...] = zero_state
        for s in range(NS - 1):

            @pl.when(s < ms)
            def _(s=s):
                states(0).wait_recv(in_f.at[s], s)
                carry_f[...] = jnp.exp2(in_tot[s] * rate2) * carry_f[...] + in_f[s].astype(F32)

    def backward_carry():
        carry_b[...] = zero_state
        for s in range(NS - 1, 0, -1):

            @pl.when(s > ms)
            def _(s=s):
                states(1).wait_recv(in_b.at[s], s)
                carry_b[...] = jnp.exp2(in_tot[s] * rate2) * carry_b[...] + in_b[s].astype(F32)

    def forward_block(hf, k, h):
        first = k * GROUP
        drives = rows_from(drive, first, GROUP, HALVES[hf])
        decays, b_rows = states_from(a_buf, first, GROUP, HALVES[hf]), states_from(bB, first, GROUP)
        later = h_buf[hf].at[pl.ds(pl.multiple_of(first * N + N, N), GROUP * N), :]
        for j in range(GROUP):
            h = state(decays, j) * h + row(drives, j) * wide(b_rows, j, HC)
            later[j * N : (j + 1) * N, :] = h.astype(BF16)
        return h

    def start_states(hf):
        start = carry_f[:, HALVES[hf]]
        h_buf[hf][:N, :] = start.astype(BF16)
        return start

    def state_rows(hf, k):
        return h_buf[hf][pl.ds(pl.multiple_of(k * GN + N, N), GN), :]

    def adjoint_rows(buf, k):
        return buf[pl.ds(pl.multiple_of(k * GN, GN), GN), :]

    def backward_block(hf, k, g):
        sl = HALVES[hf]
        first = k * GROUP
        grads = rows_from(gy, first, GROUP, sl)
        befores, lams, has = (states_from(ref[hf], first, GROUP) for ref in (h_buf, lam_buf, ha_buf))
        decays = states_from(a_buf, first, GROUP, sl)
        c_rows = states_from(cB, first, GROUP)
        for j in reversed(range(GROUP)):
            lam = row(grads, j) * wide(c_rows, j, HC) + g
            g = state(decays, j) * lam
            hold = g * state(befores, j).astype(F32)
            lams[j * N : (j + 1) * N, :] = lam.astype(BF16)
            has[j * N : (j + 1) * N, :] = (hold * rates[hf]).astype(BF16)
        return g

    def state_sums(hf, k):
        lam_rows = adjoint_rows(lam_buf[hf], k)
        adj_b = dot(b_diag[tokens(k), :], lam_rows)
        by_rate = dot(dmask[:GROUP, :].astype(BF16), adjoint_rows(ha_buf[hf], k))
        return adj_b, by_rate, dot_nt(drive[tokens(k), HALVES[hf]].astype(BF16), lam_rows)

    def c_sums(hf, k):
        return dot_nt(gy[tokens(k), HALVES[hf]].astype(BF16), state_rows(hf, k))

    def half_grads(hf, at, adj_b, by_rate):
        sl = HALVES[hf]
        pre = (by_rate + adj_b * u_bf[at, sl].astype(F32)) * jax.nn.sigmoid(pre_soft[at, sl])
        pregrad[at, sl] = pre
        prehalf[at, sl] = pre.astype(BF16)
        uscan[at, sl] = ds_ref[:, sl] * gy[at, sl] + delta[at, sl] * adj_b

    widen(bB, m_b)
    st_f[...] = lax.fori_loop(0, NB, forward_part, zero_state).astype(BF16)
    for d in range(NS - 1, 0, -1):

        @pl.when(ms + d < NS)
        def _(d=d):
            states(0).send(st_f, in_f.at[ms], ms + d)

    widen(cB, m_c)
    st_b[...] = lax.fori_loop(0, NB, backward_part, zero_state).astype(BF16)
    for d in range(NS - 1, 0, -1):

        @pl.when(ms - d >= 0)
        def _(d=d):
            states(1).send(st_b, in_b.at[ms], ms - d)

    act_slope[...] = silu_grad(pre_act[...])
    mask = (iota((T, GN), 1) // N == iota((T, GN), 0) % GROUP).astype(F32)
    b_diag[...] = (dot(ag1[:, R:], sel_b[...]) * mask).astype(BF16)
    c_diag[...] = (dot(ag1[:, R:], sel_c[...]) * mask).astype(BF16)

    def states_both(i, carry):
        g, h = carry
        for k in range(4):
            k = 4 * i + k
            c_all[tokens(k), :] = c_sums(0, k)
            g, h = backward_block(0, NB - 1 - k, g), forward_block(1, k, h)
        return g, h

    forward_carry()
    def states_first(i, h):
        for k in range(4):
            h = forward_block(0, 4 * i + k, h)
        return h

    lax.fori_loop(0, NB // 4, states_first, start_states(0))
    backward_carry()
    lax.fori_loop(0, NB // 4, states_both, (carry_b[:, HALVES[0]], start_states(1)))
    CT = CHUNK * GROUP

    def backward_chunk(i, g):
        c = NB // CHUNK - 1 - i

        def backward_second(m, g):
            k = c * CHUNK + CHUNK - 1 - m
            at = tokens(k)
            adj_all[at, :], by_all[at, :], b_all[at, :] = state_sums(0, k)
            c_all[at, :] = c_all[at, :] + c_sums(1, k)
            return backward_block(1, k, g)

        for m in range(CHUNK):
            g = backward_second(m, g)
        at = tokens(c, CT)
        sums = [state_sums(1, c * CHUNK + k) for k in range(CHUNK)]
        half_grads(0, at, adj_all[at, :], by_all[at, :])
        b_cols = (c_all[at, :] * dmask[...]).astype(BF16)
        tail = dot(b_cols, back_c[...])
        adj_b, by_rate, b_sums = (jnp.concatenate(parts, 0) for parts in zip(*sums))
        half_grads(1, at, adj_b, by_rate)
        b_cols = ((b_all[at, :] + b_sums) * dmask[...]).astype(BF16)
        tail = tail + dot(b_cols, back_b[...])
        normed = dot_nt(prehalf[at, :], dw_ref[...])
        part[at, :R] = normed
        part[at, R:] = tail
        send2[at, :R] = normed.astype(BF16)
        send2[at, R:] = tail.astype(BF16)
        for k in range(CHUNK):
            owner = c * CHUNK + k

            @pl.when(owner != mc)
            def _(owner=owner):
                chan(2).send(block(send2, owner, ROWS), rs2.at[mc], owner)

        return g

    lax.fori_loop(0, NB // CHUNK, backward_chunk, carry_b[:, HALVES[1]])

    dw_f[...] = dot_tn(ag1[:, :R], prehalf[...])
    dw_send[...] = dw_f[...].astype(BF16)
    scatter(seq(0), dw_send, dw_rs, RB)

    def outputs(i, carry):
        y = []
        for k in range(CHUNK):
            k = i * CHUNK + k
            y.append(jnp.concatenate([dot(c_diag[tokens(k), :], state_rows(hf, k)) for hf in range(2)], 1))
        at = tokens(i, CT)
        y = jnp.concatenate(y, 0) + ds_ref[...] * u_bf[at, :].astype(F32)
        zg_v[at, :] = (gz[at, :] * y).astype(BF16)
        return carry

    lax.fori_loop(0, NB // CHUNK, outputs, 0)
    leave = [pltpu.make_async_copy(v, o, s_out.at[k]) for k, (v, o) in enumerate(((zg_v, zg_o), (xg_v, xg_o), (dw_ag, dw_o)))]
    leave[0].start()

    for hf in range(2):

        def rate_part(i, acc):
            steps = rows_from(delta, i * GROUP, GROUP, HALVES[hf])
            has = states_from(ha_buf[hf], i * GROUP, GROUP)
            for j in range(GROUP):
                acc = acc + row(steps, j) * state(has, j).astype(F32)
            return acc

        sm_f[2 * N : 3 * N, HALVES[hf]] = lax.fori_loop(0, NB, rate_part, zero_state[:, :HC])
    sm_f[3 * N :, :] = jnp.zeros((SM - 3 * N, C), F32)
    sm_f[3 * N + 5 : 3 * N + 6, :] = jnp.sum(pregrad[...], 0, keepdims=True)
    sm_f[3 * N + 6 : 3 * N + 7, :] = jnp.sum(gy[...] * u_bf[...].astype(F32), 0, keepdims=True)

    grad_rows = collect(chan(2), rs2, my_rows(part))
    low = low_own[...]
    inv = inv_own[:, :1]
    scaled = grad_rows[:, :R] * dg_ref[...]
    low_grad = inv * scaled - low * (inv * inv * inv) * jnp.mean(scaled * low, -1, keepdims=True)
    gain = jnp.sum(grad_rows[:, :R] * low * inv, 0, keepdims=True)
    half = LANES // 2
    lanes = iota((ROWS, LANES), 1)
    rows = iota((ROWS, LANES), 0)
    g0 = jnp.broadcast_to(gain[:, :LANES], (ROWS, LANES))
    g1 = jnp.broadcast_to(gain[:, LANES:], (ROWS, LANES))
    q = rows % 4
    gq = jnp.where(q == 0, pltpu.roll(g0, half, 1), jnp.where(q == 1, g0, jnp.where(q == 2, pltpu.roll(g1, half, 1), g1)))
    g_hi = gq.astype(BF16).astype(F32)
    g_rows = jnp.where(rows < 4, g_hi, jnp.where(rows < 8, gq - g_hi, 0.0))
    ag2[mine, :R] = low_grad.astype(BF16)
    ag2[mine, R:] = jnp.where(lanes < half, grad_rows[:, R:], g_rows).astype(BF16)
    spread(chan(3), ag2, ROWS)

    own = collect(seq(0), dw_rs, dw_f[pl.ds(pl.multiple_of(ms * RB, RB), RB), :])
    dw_ag[pl.ds(pl.multiple_of(ms * RB, RB), RB), :] = own.astype(BF16)
    spread(seq(1), dw_ag, RB)

    arrive(chan(3), ag2, ROWS)

    PB = RB // 2

    def piece(ref, i, p):
        return ref.at[pl.ds(pl.multiple_of(i * RB + p * PB, PB), PB), :]

    xl_f[...] = dot_tn(ag2[...], u_bf[...])
    xl_send[...] = xl_f[:R, :].astype(BF16)
    for p in range(2):
        for peer in seq(2 + p).peers():
            seq(2 + p).send(piece(xl_send, peer, p), xl_rs.at[p, ms], peer)
    sm_f[: 2 * N, :] = xl_f[R:P2, :]
    total = uscan[...] + dot(ag2[:, :R], xw_ref[:R, :]) + dot(ag2[:, R:P2], xw_ref[R:, :])
    apad[:T, :] = total * act_slope[...]
    apad[T:, :] = jnp.zeros((8, C), F32)

    @pl.when(ms > 0)
    def _():
        halo_copy(apad.at[:8, :], halo_a, 1, before).start()

    sums = [jnp.zeros((16, C), F32) for _ in range(5)]
    for r in range(0, T, 16):
        grad = apad[r : r + 16, :]
        for k in range(3):
            sums[k] = sums[k] + grad * shifted[k * T + r : k * T + r + 16, :].astype(F32)
        sums[3] = sums[3] + grad * x_ref[r : r + 16, :].astype(F32)
        sums[4] = sums[4] + grad
    for k in range(5):
        sm_f[3 * N + k : 3 * N + k + 1, :] = jnp.sum(sums[k], 0, keepdims=True)
    g_sum = jnp.zeros((ROWS, LANES), F32)
    for c in range(NC):
        g_sum = g_sum + ag2[c * ROWS : (c + 1) * ROWS, R:].astype(F32)
    gq = g_sum[:4] + g_sum[4:8]
    low_half = iota((1, LANES), 1) < half
    for k in range(2):
        sm_f[3 * N + 7 : 3 * N + 8, k * LANES : (k + 1) * LANES] = jnp.where(
            low_half, pltpu.roll(gq[2 * k : 2 * k + 1], half, 1), gq[2 * k + 1 : 2 * k + 2]
        )
    for k in range(2):
        sm_own[k * SM : (k + 1) * SM, :] = sm_f[:, k * HC : (k + 1) * HC]
    sm_send[...] = sm_own[...].astype(BF16)
    scatter(seq(4), sm_send, sm_rs, SB)

    @pl.when(ms < NS - 1)
    def _():
        halo_copy(halo_a, halo_a, 1, after).wait_recv()
        apad[T:, :] = halo_a[...]

    for r in range(0, T, 32):
        total = cw[3:4] * apad[r : r + 32, :]
        for k in range(3):
            total = total + cw[k : k + 1] * apad[r + 3 - k : r + 3 - k + 32, :]
        xg_v[r : r + 32, :] = total.astype(BF16)
    leave[1].start()
    arrive(seq(1), dw_ag, RB)
    leave[2].start()

    for k, size, src in ((0, ROWS, send1), (1, ROWS, ag1), (2, ROWS, send2), (3, ROWS, ag2), (4, ROWS, send1)):
        for peer in chan(k).peers():
            if k == 0:
                pl.when(peer != 0)(functools.partial(chan(k).wait_send, src.at[:size, :], peer))
            elif k == 1:
                pl.when(mc != 0)(functools.partial(chan(k).wait_send, src.at[:size, :], peer))
            else:
                chan(k).wait_send(src.at[:size, :], peer)
    for k, src in ((0, dw_send), (1, dw_ag)):
        for peer in seq(k).peers():
            seq(k).wait_send(src.at[:RB, :], peer)
    for peer in states(2).peers():
        states(2).wait_send(tot, peer)
    for d in range(1, NS):

        @pl.when(ms + d < NS)
        def _(d=d):
            states(0).wait_send(st_f, ms + d)

        @pl.when(ms - d >= 0)
        def _(d=d):
            states(1).wait_send(st_b, ms - d)

    @pl.when(ms < NS - 1)
    def _():
        halo_copy(halo_x, halo_x, 0, after).wait_send()

    @pl.when(ms > 0)
    def _():
        halo_copy(halo_a, halo_a, 1, before).wait_send()

    for p in range(2):
        at = pl.ds(pl.multiple_of(ms * RB + p * PB, PB), PB)
        xl_ag[at, :] = collect(seq(2 + p), xl_rs.at[p], xl_f[at, :]).astype(BF16)
        for peer in seq(5 + p).peers():
            seq(5 + p).send(piece(xl_ag, ms, p), piece(xl_ag, ms, p), peer)
    at = pl.ds(pl.multiple_of(ms * SB, SB), SB)
    sm_ag[at, :] = collect(seq(4), sm_rs, sm_own[at, :]).astype(BF16)
    spread(seq(7), sm_ag, SB)
    for copy in leave:
        copy.wait()
    for k, size, src in ((2, PB, xl_send), (3, PB, xl_send), (4, SB, sm_send)):
        for peer in seq(k).peers():
            seq(k).wait_send(src.at[:size, :], peer)
    for p in range(2):
        for peer in seq(5 + p).peers():
            seq(5 + p).wait_recv(piece(xl_ag, peer, p), peer)
    arrive(seq(7), sm_ag, SB)
    for k, size, src in ((5, PB, xl_ag), (6, PB, xl_ag), (7, SB, sm_ag)):
        for peer in seq(k).peers():
            seq(k).wait_send(src.at[:size, :], peer)


def finish_kernel(dims, xg, zg, dw_sum, xl_sum, sm_sum, xg_o, zg_o, cwg_o, cbg_o, xpg_o, dwg_o, dbg_o, alg_o, dsg_o, dgg_o):
    T, C, NS, NC, R, N = dims
    scale = 1.0 / math.sqrt(T * NS)
    xg_o[...] = xg[...]
    zg_o[...] = zg[...]
    dwg_o[...] = scale * dw_sum[...].astype(F32)
    xpg_o[:R, :] = scale * xl_sum[...].astype(F32)
    HC = C // 2
    small = scale * sm_sum[...].astype(F32)
    for hf in range(2):
        sl = slice(hf * HC, (hf + 1) * HC)
        rows = small[hf * 4 * N : (hf + 1) * 4 * N]
        xpg_o[R:, sl] = rows[: 2 * N]
        alg_o[:, sl] = rows[2 * N : 3 * N]
        cwg_o[:, sl] = rows[3 * N : 3 * N + 4]
        cbg_o[:, sl] = rows[3 * N + 4 : 3 * N + 5]
        dbg_o[:, sl] = rows[3 * N + 5 : 3 * N + 6]
        dsg_o[:, sl] = rows[3 * N + 6 : 3 * N + 7]
        if hf * HC < R:
            dgg_o[:, sl] = rows[3 * N + 7 : 3 * N + 8]


def per_device(counts, x_in, z_in, grad_out, conv_w, conv_b, xproj_w, dt_w, dt_bias, a_log, d_skip, dt_gain):
    T, C = x_in.shape
    R = dt_w.shape[0]
    N = a_log.shape[1]
    NS, NC = counts
    ROWS = T // NC
    W = R + LANES
    GN = GROUP * N
    SM = 4 * N
    HC = C // 2
    dims = (T, C, NS, NC, R, N)

    def f32(*shape):
        return pltpu.VMEM(shape, F32)

    def b16(*shape):
        return pltpu.VMEM(shape, BF16)

    dma = pltpu.SemaphoreType.DMA
    scratch = dict(
        x_ref=b16(T, C), z_ref=b16(T, C), g_ref=b16(T, C), cw_ref=f32(4, C), cb_ref=f32(1, C), xw_ref=b16(R + 2 * N, C),
        dw_ref=b16(R, C), db_ref=f32(1, C), al_ref=f32(N, C), ds_ref=f32(1, C), dg_ref=f32(1, R),
        xg_v=b16(T, C), zg_v=b16(T, C), dw_ag=b16(R, C), shifts=b16(3 * T, T), shifted=b16(3 * T, C),
        first_parts=b16(NC, ROWS, W), pre_act=f32(T, C), act_slope=f32(T, C), u_bf=b16(T, C), gy=f32(T, C), gz=f32(T, C),
        part=f32(T, W), send1=b16(T, W), rs1=b16(NC, ROWS, W), ag1=b16(T, W),
        low_own=f32(ROWS, R), inv_own=f32(ROWS, LANES),
        pre_soft=f32(T, C), delta=f32(T, C), drive=f32(T, C), bB=f32(T * N, LANES), cB=f32(T * N, LANES),
        a_buf=f32(T * N, C), h0=b16((T + 1) * N, HC), h1=b16((T + 1) * N, HC),
        lam0=b16(T * N, HC), lam1=b16(T * N, HC), ha0=b16(T * N, HC), ha1=b16(T * N, HC),
        st_f=b16(N, C), st_b=b16(N, C), tot=f32(1, C), in_f=b16(NS, N, C), in_b=b16(NS, N, C),
        in_tot=f32(NS, 1, C), carry_f=f32(N, C), carry_b=f32(N, C),
        e_exp=b16(GN, GROUP), m_b=f32(GN, LANES), m_c=f32(GN, LANES), sel_b=b16(LANES, GN), sel_c=b16(LANES, GN),
        dmask=f32(CHUNK * GROUP, GN), back_b=b16(GN, LANES), back_c=b16(GN, LANES),
        tail32=f32(T, LANES), b_diag=b16(T, GN), c_diag=b16(T, GN), b_all=f32(T, GN), c_all=f32(T, GN), adj_all=f32(T, HC), by_all=f32(T, HC),
        uscan=f32(T, C), pregrad=f32(T, C), prehalf=b16(T, C),
        send2=b16(T, W), rs2=b16(NC, ROWS, W), ag2=b16(T, W),
        dw_f=f32(R, C), dw_send=b16(R, C), dw_rs=b16(NS, R // NS, C),
        xl_f=f32(W, C), xl_send=b16(R, C), xl_rs=b16(2, NS, R // NS // 2, C),
        sm_f=f32(SM, C), sm_own=f32(2 * SM, HC), sm_send=b16(2 * SM, HC), sm_rs=b16(NS, 2 * SM // NS, HC),
        halo_x=b16(16, C), halo_a=f32(8, C), apad=f32(T + 8, C),
        s_in=dma((11,)), s_out=dma((3,)), s_c=dma((5, NC)), r_c=dma((5, NC)), s_st=dma((3, NS)), r_st=dma((3, NS)),
        s_sq=dma((8, NS)), r_sq=dma((8, NS)), s_h=dma((2,)), r_h=dma((2,)),
    )
    S = jax.ShapeDtypeStruct
    vmem = pl.BlockSpec(memory_space=pltpu.VMEM)
    raw = pl.pallas_call(
        functools.partial(layer_kernel, dims),
        out_shape=(S((T, C), BF16), S((T, C), BF16), S((R, C), BF16), S((R, C), BF16), S((2 * SM, HC), BF16)),
        in_specs=[pl.BlockSpec(memory_space=pl.ANY)] * 11,
        out_specs=(pl.BlockSpec(memory_space=pl.ANY),) * 3 + (vmem,) * 2,
        scratch_shapes=list(scratch.values()),
        compiler_params=pltpu.CompilerParams(
            collective_id=0, has_side_effects=True, vmem_limit_bytes=VMEM_BYTES
        ),
    )(
        x_in, z_in, grad_out, conv_w, conv_b[None], xproj_w.T, dt_w, dt_bias[None], a_log.T, d_skip[None], dt_gain[None],
    )
    xg, zg, cwg, cbg, xpg, dwg, dbg, alg, dsg, dgg = pl.pallas_call(
        functools.partial(finish_kernel, dims),
        out_shape=(
            S((T, C), BF16), S((T, C), BF16), S((4, C), F32), S((1, C), F32), S((R + 2 * N, C), F32),
            S((R, C), F32), S((1, C), F32), S((N, C), F32), S((1, C), F32), S((1, R), F32),
        ),
        in_specs=[vmem] * 5,
        out_specs=(vmem,) * 10,
        compiler_params=pltpu.CompilerParams(vmem_limit_bytes=VMEM_BYTES),
    )(*raw)
    return xg, zg, cwg, cbg[0], xpg.T, dwg, dbg[0], alg.T, dsg[0], dgg[0]


def solution(mesh):
    placed = (
        P("seq", "chan"),
        P("seq", "chan"),
        P("seq", "chan"),
        P(None, "chan"),
        P("chan"),
        P("chan", None),
        P(None, "chan"),
        P("chan"),
        P("chan", None),
        P("chan"),
        P(),
    )
    counts = (mesh.shape["seq"], mesh.shape["chan"])
    return jax.shard_map(
        functools.partial(per_device, counts),
        mesh=mesh,
        in_specs=placed,
        out_specs=(
            P("seq", "chan"),
            P("seq", "chan"),
            P(None, "chan"),
            P("chan"),
            P("chan", None),
            P(None, "chan"),
            P("chan"),
            P("chan", None),
            P("chan"),
            P(),
        ),
        check_vma=False,
    )
```
